512 devices in a mesh: dp: 32 (over x, y, core), expert: 16 (over z).
Axes of the slice: x: 4, y: 4, z: 16, core: 2. Of those that a mesh axis runs over, the one named last changes fastest.
Arguments:
- tokens: bfloat16 [65536, 512], P(('dp', 'expert')), may hold values from -6 to 6
- out_grad: bfloat16 [65536, 512], P(('dp', 'expert')), may hold values from -6 to 6
- probs: float32 [65536, 2], P(('dp', 'expert')), may hold values from 0.1 to 1
- routes: int32 [65536, 2], P(('dp', 'expert')), may hold values from 0 to 15, all different within a row; in each aligned block of 128 rows (0 to 127, 128 to 255, ...) at most 24 rows name the same one
- w_gate: bfloat16 [16, 512, 2048], P('expert', 'dp'), may hold values from -0.25 to 0.25
- w_up: bfloat16 [16, 512, 2048], P('expert', 'dp'), may hold values from -0.25 to 0.25
- w_down: bfloat16 [16, 2048, 512], P('expert', 'dp'), may hold values from -0.125 to 0.125
Outputs:
- token_grad: bfloat16 [65536, 512], P(('dp', 'expert'))
- gate_grad: bfloat16 [16, 512, 2048], P('expert', 'dp')
- up_grad: bfloat16 [16, 512, 2048], P('expert', 'dp')
The draws below stay inside these ranges and needn't reach their ends.
Inputs may be any that keep to these rules, and one draw needn't show every extreme that they name: `routes`: each row names two different experts; among the 128 rows of one device no expert is named more than 24 times, and in every draw some device names some expert exactly 24 times.
All inputs are finite; a program needn't handle non-finite values.
Results may differ from the reference program's by a relative error of at most 0.02.
Values may be sent and summed in bfloat16 or wider, within the bound.
A program may use at most 64 MiB of HBM per device.

```python
import math
import jax
import jax.numpy as jnp
import numpy as np
from jax import lax

D = 512
FF = 2048
TOK_DEV = 128
EXPERTS = 16
CAP = 24
TOKENS = 65536
N_DP = 32
N_EXPERT = 16


def block_levels(rng, shape, shards, smallest, largest):
    level = 1.0
    for position, shards_of in shards:
        steps = jax.random.uniform(jax.random.fold_in(jax.random.fold_in(rng, 6), position), (shards_of,), jnp.float32, smallest / len(shards), largest / len(shards))
        level = level * jnp.repeat(jnp.exp(steps), shape[position] // shards_of).reshape((-1,) + (1,) * (len(shape) - 1 - position))
    return level


def shared_out(stream_key, own, number, rows, number_of, top, most, slope):
    ranking = jax.random.permutation(stream_key, number_of)
    heavy_load, common = portions_of(number_of, rows * top, most, slope, True), portions_of(number_of, rows * top, most, slope, False)
    places = jnp.arange(number_of)

    def named(lengths, offset_by):
        used = int((lengths > 0).sum())
        fixed = max(1, used // 4)
        moved = fixed + (places - fixed + offset_by * (used - fixed)) % max(1, number_of - fixed)
        return jnp.zeros((number_of,), jnp.int32).at[ranking[jnp.where(places < fixed, places, moved)]].set(jnp.asarray(lengths, jnp.int32))

    lengths = jnp.where(number % 4 == 0, named(heavy_load, number // 4), named(common, number - number // 4 - 1))
    mixed = jax.random.permutation(jax.random.fold_in(own, 3), number_of)
    donor, taker = mixed[0:number_of // 2 * 2:2], mixed[1:number_of // 2 * 2:2]
    slack = jnp.minimum(lengths[donor] - 1, most - lengths[taker]) // 2
    slack = jnp.where((donor == ranking[0]) | (taker == ranking[0]) | (lengths[taker] == 0), 0, jnp.maximum(slack, 0))
    moved = jax.random.randint(jax.random.fold_in(own, 4), (number_of // 2,), 0, 1 << 20) % (slack + 1)
    lengths = lengths.at[donor].add(-moved).at[taker].add(moved)
    items = jnp.searchsorted(jnp.cumsum(lengths), jnp.arange(rows * top), side="right").astype(jnp.int32)
    listing = items.reshape(top, rows).T
    listing = listing[jax.random.permutation(jax.random.fold_in(own, 1), rows)]
    offset_by = jax.random.randint(jax.random.fold_in(own, 2), (rows, 1), 0, top)
    return jnp.take_along_axis(listing, (jnp.arange(top)[None, :] + offset_by) % top, axis=1)


def portions_of(number_of, total, limit, lean, full):
    weights = [(1 << 20) // math.isqrt(standing ** lean) + 1 for standing in range(1, number_of + 1)]
    largest = limit if full else min(limit, max(-(-total // number_of), total * weights[0] // sum(weights)))
    least = 1 if total - largest >= number_of - 1 else 0
    counts, spare = [largest] + [least] * (number_of - 1), total - largest - least * (number_of - 1)
    while spare > 0:
        movable = [i for i in range(1, number_of) if counts[i] < largest] or [i for i in range(1, number_of) if counts[i] < limit]
        mass, left = sum([weights[i] for i in movable]), spare
        for i in movable:
            addition = min(limit - counts[i], max(1, left * weights[i] // mass), spare)
            counts[i] = counts[i] + addition
            spare = spare - addition
    return np.array(counts)


def gaussian(key, dims, scale, most, shards=(), held_as=jnp.bfloat16):
    drawn = jax.random.normal(key, dims, jnp.float32) * scale
    if len(shards) > 0:
        drawn = block_levels(key, dims, shards, -0.22, 0.18) * drawn
    return jnp.clip(drawn, min=-most, max=most).astype(held_as)


def setup_inputs(seed: int = 0) -> dict:
    splits = jax.random.split(jax.random.key(seed), 8)
    tokens = gaussian(splits[0], (TOKENS, D), 1.0, 6.0, ((0, 512),))
    out_grad = gaussian(splits[1], (TOKENS, D), 1.0, 6.0, ((0, 512),))
    probs = jnp.clip(0.1 + 0.9 * jax.random.uniform(splits[2], (TOKENS, 2), jnp.float32) ** block_levels(splits[2], (TOKENS, 2), ((0, 512),), -0.2, 0.2), 0.1, 1.0)
    routes_keys = jax.random.split(jax.random.fold_in(splits[3], 1), TOKENS // TOK_DEV)
    routes_turns = jax.random.permutation(jax.random.fold_in(splits[3], 3), TOKENS // TOK_DEV)
    routes = jax.vmap(lambda own, number: shared_out(jax.random.fold_in(splits[3], 2), own, number, TOK_DEV, EXPERTS, 2, CAP, 2))(routes_keys, routes_turns).reshape((TOKENS, 2))
    w_gate = gaussian(splits[4], (EXPERTS, D, FF), D ** -0.5, 0.25, ((0, 16), (1, 32)))
    w_up = gaussian(splits[5], (EXPERTS, D, FF), D ** -0.5, 0.25, ((0, 16), (1, 32)))
    w_down = gaussian(splits[6], (EXPERTS, FF, D), FF ** -0.5, 0.125, ((0, 16), (1, 32)))
    return dict(tokens=tokens, out_grad=out_grad, probs=probs, routes=routes, w_gate=w_gate, w_up=w_up, w_down=w_down)


def slot_positions(block_routes):
    flat = block_routes.reshape(-1)
    onehot = (flat[:, None] == jnp.arange(EXPERTS, dtype=jnp.int32)[None, :]).astype(jnp.int32)
    before = jnp.cumsum(onehot, axis=0) - onehot
    slot = jnp.sum(before * onehot, axis=1)
    return (flat * CAP + slot).astype(jnp.int32)


def place_rows(rows, where):
    return jnp.zeros((EXPERTS * CAP, rows.shape[1]), rows.dtype).at[where].set(rows)


def expert_backward(inputs):
    xs, gs, w_g, w_u, w_d = inputs
    rows_x = xs.reshape(-1, D)
    rows_g = gs.reshape(-1, D)
    a = jnp.dot(rows_x, w_g, preferred_element_type=jnp.float32)
    c = jnp.dot(rows_x, w_u, preferred_element_type=jnp.float32)
    dh = jnp.dot(rows_g, w_d.T, preferred_element_type=jnp.float32)
    sig = jax.nn.sigmoid(a)
    da = (dh * c * sig * (1.0 + a * (1.0 - sig))).astype(jnp.bfloat16)
    dc = (dh * a * sig).astype(jnp.bfloat16)
    rows_grad = (jnp.dot(da, w_g.T, preferred_element_type=jnp.float32)
                 + jnp.dot(dc, w_u.T, preferred_element_type=jnp.float32)).astype(jnp.bfloat16)
    xf = xs.astype(jnp.float32)
    gate_terms = jnp.einsum('jrd,jrf->jdf', xf, da.reshape(N_DP, -1, FF).astype(jnp.float32)).astype(jnp.bfloat16)
    up_terms = jnp.einsum('jrd,jrf->jdf', xf, dc.reshape(N_DP, -1, FF).astype(jnp.float32)).astype(jnp.bfloat16)
    gate_sum = jnp.sum(gate_terms.astype(jnp.float32), axis=0).astype(jnp.bfloat16)
    up_sum = jnp.sum(up_terms.astype(jnp.float32), axis=0).astype(jnp.bfloat16)
    return rows_grad.reshape(N_DP, -1, D), gate_sum, up_sum


def reference(tokens, out_grad, probs, routes, w_gate, w_up, w_down):
    blocks = N_DP * N_EXPERT
    where = jax.vmap(slot_positions)(routes.reshape(blocks, TOK_DEV, 2))
    token_rows = jnp.repeat(tokens, 2, axis=0).reshape(blocks, 2 * TOK_DEV, D)
    scaled = (out_grad.astype(jnp.float32)[:, None, :] * probs[:, :, None]).astype(jnp.bfloat16)
    scaled = scaled.reshape(blocks, 2 * TOK_DEV, D)
    sent_x = jax.vmap(place_rows)(token_rows, where)
    sent_g = jax.vmap(place_rows)(scaled, where)

    def by_expert(sent):
        grid = sent.reshape(N_DP, N_EXPERT, EXPERTS, CAP, D)
        return jnp.transpose(grid, (2, 0, 1, 3, 4)).reshape(EXPERTS, N_DP, N_EXPERT * CAP, D)

    rows_grad, gate_grad, up_grad = lax.map(expert_backward, (by_expert(sent_x), by_expert(sent_g), w_gate, w_up, w_down))
    back = rows_grad.reshape(EXPERTS, N_DP, N_EXPERT, CAP, D)
    back = jnp.transpose(back, (1, 2, 0, 3, 4)).reshape(blocks, EXPERTS * CAP, D)
    picked = jnp.take_along_axis(back, where[:, :, None], axis=1)
    token_grad = jnp.sum(picked.astype(jnp.float32).reshape(TOKENS, 2, D), axis=1).astype(jnp.bfloat16)
    return token_grad, gate_grad, up_grad
```

```python
import functools

import jax
import jax.numpy as jnp
from jax import lax
from jax.experimental import pallas as pl
from jax.experimental.pallas import tpu as pltpu
from jax.sharding import PartitionSpec as P

MESH = pl.DeviceIdType.MESH
F32 = jnp.float32
BF16 = jnp.bfloat16
NN = (((1,), (0,)), ((), ()))
NT = (((1,), (1,)), ((), ()))
TN = (((0,), (0,)), ((), ()))


def dot(a, b, dims):
    return lax.dot_general(a, b, dims, preferred_element_type=F32)


def kernel(
    nx, ny, nz, groups, cap,
    tokens_ref, grad_ref, probs_ref, routes_ref, gate_ref, up_ref, down_ref,
    token_out, gate_out, up_out,
    sel, send, recv, wg, wu, wd, stage, xall, daall, dcall, own_part, sib_out, sib_in, ret, back,
    gterm, uterm, gin1, uin1, gmid, umid, gin2, uin2, swap_out, swap_in,
    z_send, z_recv, f_send, f_recv, w0_send, w0_recv, w1_send, w1_recv, w2_send, w2_recv,
    p_send, p_recv, b_send, b_recv, r1_send, r1_recv, r2_send, r2_recv, r3_send, r3_recv,
):
    dp = lax.axis_index("dp")
    z = lax.axis_index("expert")
    chip = dp // 2
    core = lax.rem(dp, 2)
    x = chip // ny
    y = lax.rem(chip, ny)
    tok, width = tokens_ref.shape
    rows_of = gate_ref.shape[0]
    ff = gate_ref.shape[1]
    fh = ff // 2
    down_rows = down_ref.shape[0]
    half_down = down_rows // 2
    per = nz // groups
    tile = ny * down_rows
    half_width = width // 2
    crows = 2 * rows_of

    sibling = (chip * 2 + (1 - core), z)

    def at_x(j):
        other = lax.rem(x + j, nx)
        return other, ((other * ny + y) * 2 + core, z)

    def at_y(j):
        other = lax.rem(y + j, ny)
        return other, ((x * ny + other) * 2 + core, z)

    def offset(pos):
        i = pos // 2
        return nz // 2 + i * (2 * lax.rem(pos, 2) - 1)

    def remote(src, dst, send_sem, recv_sem, device):
        return pltpu.make_async_remote_copy(
            src_ref=src, dst_ref=dst, send_sem=send_sem, recv_sem=recv_sem,
            device_id=device, device_id_type=MESH,
        )

    barrier = pltpu.get_barrier_semaphore()

    def greet(device):
        pl.semaphore_signal(barrier, inc=1, device_id=device, device_id_type=MESH)

    greet(sibling)
    for j in range(1, nx):
        greet(at_x(j)[1])
    for j in range(1, ny):
        greet(at_y(j)[1])

    def greet_z(k, carry):
        greet((dp, lax.rem(z + k, nz)))
        return carry

    lax.fori_loop(1, nz, greet_z, 0)

    lanes = lax.broadcasted_iota(jnp.int32, (rows_of, 128), 1) < 64
    for which, (ref, full) in enumerate(((gate_ref, wg), (up_ref, wu))):
        for j in range(fh // 128):
            even = ref[:, 256 * j:256 * j + 128].astype(F32)
            odd = ref[:, 256 * j + 128:256 * j + 256].astype(F32)
            low = jnp.where(lanes, even, pltpu.roll(odd, 64, 1))
            high = jnp.where(lanes, pltpu.roll(even, 64, 1), odd)
            full[x, y, core, :, 128 * j:128 * j + 128] = jnp.where(core == 0, low, high).astype(BF16)
            stage[which, :, 128 * j:128 * j + 128] = jnp.where(core == 0, high, low).astype(BF16)
    wd[x, y] = down_ref[...]

    experts = lax.broadcasted_iota(jnp.int32, (nz, tok), 0)
    first = routes_ref[0:1, :]
    second = routes_ref[1:2, :]
    is_first = (experts == first).astype(F32)
    is_second = (experts == second).astype(F32)
    earlier = (
        lax.broadcasted_iota(jnp.int32, (tok, tok), 0) < lax.broadcasted_iota(jnp.int32, (tok, tok), 1)
    ).astype(F32).astype(BF16)
    before = dot((is_first + is_second).astype(BF16), earlier, NN)
    place_first = first.astype(F32) * cap + jnp.sum(before * is_first, axis=0, keepdims=True)
    place_second = second.astype(F32) * cap + jnp.sum(before * is_second, axis=0, keepdims=True)
    slots = lax.broadcasted_iota(jnp.int32, (nz * cap, tok), 0).astype(F32)
    in_first = (slots == place_first).astype(F32)
    in_second = (slots == place_second).astype(F32)
    weight = jnp.sum(in_first * probs_ref[0:1, :] + in_second * probs_ref[1:2, :], axis=1, keepdims=True)
    sel[...] = (in_first + in_second).astype(BF16)
    rows_x = dot(sel[...], tokens_ref[...], NN).reshape(nz, cap, width)
    rows_g = (dot(sel[...], grad_ref[...], NN) * weight).reshape(nz, cap, width)
    send[...] = jnp.concatenate([rows_x, rows_g], axis=1).astype(BF16)
    recv[0, 0] = send[z]

    pl.semaphore_wait(barrier, nz + nx + ny - 2)

    def w0(which):
        full = (wg, wu)[which]
        return remote(stage.at[which], full.at[x, y, core], w0_send.at[which], w0_recv.at[which], sibling)

    def w1(array, j):
        along_x = array in (0, 2)
        other, device = at_x(j) if along_x else at_y(j)
        if array == 0:
            ref = wg.at[x, y]
        elif array == 1:
            ref = wu.at[x, y]
        elif array == 2:
            ref = wd.at[x, y, pl.ds(0, half_down)]
        else:
            ref = wd.at[x, y, pl.ds(half_down, half_down)]
        return remote(ref, ref, w1_send.at[array, j], w1_recv.at[array, j], device)

    def w2(array, j):
        along_x = array in (1, 3)
        other, device = at_x(j) if along_x else at_y(j)
        if array == 0:
            ref = wg.at[:, y]
        elif array == 1:
            ref = wu.at[x]
        elif array == 2:
            ref = wd.at[:, y, pl.ds(0, half_down)]
        else:
            ref = wd.at[x, :, pl.ds(half_down, half_down)]
        return remote(ref, ref, w2_send.at[array, j], w2_recv.at[array, j], device)

    def peers1(array):
        return range(1, nx if array in (0, 2) else ny)

    def peers2(array):
        return range(1, nx if array in (1, 3) else ny)

    for which in range(2):
        w0(which).start()
    for array in (2, 3):
        for j in peers1(array):
            w1(array, j).start()

    def z_copy(pos):
        other = lax.rem(z + offset(pos), nz)
        return remote(send.at[other], recv.at[0, pos], z_send.at[pos], z_recv.at[pos], (dp, other))

    def z_start(pos, carry):
        z_copy(pos).start()
        return carry

    lax.fori_loop(1, nz, z_start, 0)

    for which in range(2):
        w0(which).wait_recv()
        for j in peers1(which):
            w1(which, j).start()
    for array in range(4):
        for j in peers1(array):
            w1(array, j).wait_recv()
        for j in peers2(array):
            w2(array, j).start()

    def f_copy(pos):
        return remote(recv.at[0, pos], recv.at[1, pos], f_send.at[pos], f_recv.at[pos], sibling)

    def forward(group):
        def one(pos, carry):
            z_copy(pos).wait_recv()
            f_copy(pos).start()
            return carry

        if group == 0:
            f_copy(0).start()
        lax.fori_loop(max(group * per, 1), group * per + per, one, 0)

    def f_wait(group):
        def one(pos, carry):
            f_copy(pos).wait_recv()
            return carry

        lax.fori_loop(group * per, group * per + per, one, 0)

    def p_copy(group):
        return remote(sib_out.at[group], sib_in.at[group], p_send.at[group], p_recv.at[group], sibling)

    def work(group):
        f_wait(group)
        got = recv[:, group * per:group * per + per].astype(F32)
        gx = got[:, :, :cap].reshape(2 * per * cap, width).astype(BF16)
        gg = got[:, :, cap:].reshape(2 * per * cap, width).astype(BF16)
        xall[group] = gx

        def step(t, total):
            cols = pl.ds(pl.multiple_of(t * tile, tile), tile)
            w_g = wg[:, :, :, :, cols].reshape(width, tile)
            w_u = wu[:, :, :, :, cols].reshape(width, tile)
            w_d = wd[t].reshape(tile, width)
            a = dot(gx, w_g, NN)
            c = dot(gx, w_u, NN)
            dh = dot(gg, w_d, NT)
            s = jax.nn.sigmoid(a)
            da = (dh * c * s * (1.0 + a * (1.0 - s))).astype(BF16)
            dc = (dh * a * s).astype(BF16)
            daall[group, :, cols] = da
            dcall[group, :, cols] = dc
            return total + dot(da, w_g, NT) + dot(dc, w_u, NT)

        total = lax.fori_loop(0, fh // tile, step, jnp.zeros((2 * per * cap, width), F32))
        own_part[group] = total[:per * cap]
        sib_out[group] = total[per * cap:]
        p_copy(group).start()

    def b_copy(pos):
        other = lax.rem(z + nz - offset(pos), nz)
        return remote(ret.at[pos], back.at[z], b_send.at[pos], b_recv.at[z], (dp, other))

    def b_wait(other):
        return remote(ret.at[0], back.at[other], b_send.at[0], b_recv.at[other], (dp, other))

    def give_back(group):
        p_copy(group).wait_recv()
        rows = (own_part[group] + sib_in[group]).reshape(per, cap, width)
        ret[group * per:group * per + per] = jnp.concatenate(
            [rows[:, :, :half_width], rows[:, :, half_width:]], axis=1
        ).astype(BF16)

        def one(pos, carry):
            b_copy(pos).start()
            return carry

        if group == 0:
            back[z] = ret[0]
        lax.fori_loop(max(group * per, 1), group * per + per, one, 0)

    for group in range(groups - 1):
        forward(group)
    for array in range(4):
        for j in peers2(array):
            w2(array, j).wait_recv()
    for group in range(groups):
        if group == groups - 1:
            forward(group)
        work(group)
        if group > 0:
            give_back(group - 1)
    give_back(groups - 1)

    rows_all = groups * 2 * per * cap
    along = ny * crows

    def term(ref, i):
        cols = pl.ds(pl.multiple_of(i * along, along), along)
        xs = xall[:, :, cols].reshape(rows_all, along)
        return dot(xs, ref[...].reshape(rows_all, fh), TN)

    def r1_gate(j):
        other, device = at_x(j)
        return remote(gterm.at[other], gin1.at[j], r1_send.at[0, j], r1_recv.at[0, j], device)

    def r1_up(j):
        other, device = at_y(j)
        return remote(uterm.at[:, other], uin1.at[j], r1_send.at[1, j], r1_recv.at[1, j], device)

    def gate_step(j, carry):
        other = lax.rem(x + j, nx)
        gterm[other] = term(daall, other).reshape(ny, crows, fh).astype(BF16)
        r1_gate(j).start()
        return carry

    lax.fori_loop(1, nx, gate_step, 0)

    def up_step(i, carry):
        uterm[i] = term(dcall, i).reshape(ny, crows, fh).astype(BF16)
        return carry

    lax.fori_loop(0, nx, up_step, 0)
    for j in range(1, ny):
        r1_up(j).start()
    gterm[x] = term(daall, x).reshape(ny, crows, fh).astype(BF16)

    def r2_gate(j):
        other, device = at_y(j)
        return remote(gmid.at[other], gin2.at[j], r2_send.at[0, j], r2_recv.at[0, j], device)

    def r2_up(j):
        other, device = at_x(j)
        return remote(umid.at[other], uin2.at[j], r2_send.at[1, j], r2_recv.at[1, j], device)

    for j in range(1, nx):
        r1_gate(j).wait_recv()

    def gate_sum(i, carry):
        total = gterm[x, i].astype(F32)
        for j in range(1, nx):
            total = total + gin1[j, i].astype(F32)
        gmid[i] = total.astype(BF16)
        return carry

    lax.fori_loop(0, ny, gate_sum, 0)
    for j in range(1, ny):
        r2_gate(j).start()
    for j in range(1, ny):
        r1_up(j).wait_recv()

    def up_sum(i, carry):
        total = uterm[i, y].astype(F32)
        for j in range(1, ny):
            total = total + uin1[j, i].astype(F32)
        umid[i] = total.astype(BF16)
        return carry

    lax.fori_loop(0, nx, up_sum, 0)
    for j in range(1, nx):
        r2_up(j).start()

    def r3(which):
        return remote(swap_out.at[which], swap_in.at[which], r3_send.at[which], r3_recv.at[which], sibling)

    mine = []
    for which, (mid, place, came, copies, count) in enumerate(
        ((gmid, y, gin2, r2_gate, ny), (umid, x, uin2, r2_up, nx))
    ):
        for j in range(1, count):
            copies(j).wait_recv()
        total = mid[place].astype(F32)
        for j in range(1, count):
            total = total + came[j].astype(F32)
        mine.append(jnp.where(core == 0, total[:rows_of], total[rows_of:]))
        swap_out[which] = jnp.where(core == 0, total[rows_of:], total[:rows_of]).astype(BF16)
        r3(which).start()

    def back_wait(k, carry):
        b_wait(lax.rem(z + k, nz)).wait_recv()
        return carry

    lax.fori_loop(1, nz, back_wait, 0)
    came = back[...].astype(F32)
    came = jnp.concatenate([came[:, :cap], came[:, cap:]], axis=2).reshape(nz * cap, width).astype(BF16)
    token_out[...] = dot(sel[...], came, TN).astype(BF16)

    for which, out in enumerate((gate_out, up_out)):
        r3(which).wait_recv()
        theirs = swap_in[which].astype(F32)
        half0 = jnp.where(core == 0, mine[which], theirs)
        half1 = jnp.where(core == 0, theirs, mine[which])
        for j in range(fh // 128):
            h0 = half0[:, 128 * j:128 * j + 128]
            h1 = half1[:, 128 * j:128 * j + 128]
            out[:, 256 * j:256 * j + 128] = jnp.where(lanes, h0, pltpu.roll(h1, 64, 1)).astype(BF16)
            out[:, 256 * j + 128:256 * j + 256] = jnp.where(lanes, pltpu.roll(h0, 64, 1), h1).astype(BF16)

    for which in range(2):
        w0(which).wait_send()
        r3(which).wait_send()
    for array in range(4):
        for j in peers1(array):
            w1(array, j).wait_send()
        for j in peers2(array):
            w2(array, j).wait_send()
    for group in range(groups):
        p_copy(group).wait_send()
    f_copy(0).wait_send()

    def drain(pos, carry):
        z_copy(pos).wait_send()
        f_copy(pos).wait_send()
        b_copy(pos).wait_send()
        return carry

    lax.fori_loop(1, nz, drain, 0)
    for j in range(1, nx):
        r1_gate(j).wait_send()
        r2_up(j).wait_send()
    for j in range(1, ny):
        r1_up(j).wait_send()
        r2_gate(j).wait_send()


def body(nx, ny, nz, groups, cap, tokens, out_grad, probs, routes, w_gate, w_up, w_down):
    tok, width = tokens.shape
    rows_of, ff = w_gate.shape[1:]
    down_rows = w_down.shape[1]
    fh = ff // 2
    per = nz // groups
    crows = 2 * rows_of
    vmem = pltpu.VMEM
    dma = pltpu.SemaphoreType.DMA
    most = max(nx, ny)
    return pl.pallas_call(
        functools.partial(kernel, nx, ny, nz, groups, cap),
        out_shape=(
            jax.ShapeDtypeStruct((tok, width), BF16),
            jax.ShapeDtypeStruct((rows_of, ff), BF16),
            jax.ShapeDtypeStruct((rows_of, ff), BF16),
        ),
        in_specs=[pl.BlockSpec(memory_space=pltpu.VMEM)] * 7,
        out_specs=(pl.BlockSpec(memory_space=pltpu.VMEM),) * 3,
        scratch_shapes=[
            vmem((nz * cap, tok), BF16),
            vmem((nz, 2 * cap, width), BF16),
            vmem((2, nz, 2 * cap, width), BF16),
            vmem((nx, ny, 2, rows_of, fh), BF16),
            vmem((nx, ny, 2, rows_of, fh), BF16),
            vmem((nx, ny, down_rows, width), BF16),
            vmem((2, rows_of, fh), BF16),
            vmem((groups, 2 * per * cap, width), BF16),
            vmem((groups, 2 * per * cap, fh), BF16),
            vmem((groups, 2 * per * cap, fh), BF16),
            vmem((groups, per * cap, width), F32),
            vmem((groups, per * cap, width), F32),
            vmem((groups, per * cap, width), F32),
            vmem((nz, 2 * cap, width // 2), BF16),
            vmem((nz, 2 * cap, width // 2), BF16),
            vmem((nx, ny, crows, fh), BF16),
            vmem((nx, ny, crows, fh), BF16),
            vmem((nx, ny, crows, fh), BF16),
            vmem((ny, nx, crows, fh), BF16),
            vmem((ny, crows, fh), BF16),
            vmem((nx, crows, fh), BF16),
            vmem((ny, crows, fh), BF16),
            vmem((nx, crows, fh), BF16),
            vmem((2, rows_of, fh), BF16),
            vmem((2, rows_of, fh), BF16),
            dma((nz,)), dma((nz,)), dma((nz,)), dma((nz,)),
            dma((2,)), dma((2,)), dma((4, most)), dma((4, most)), dma((4, most)), dma((4, most)),
            dma((groups,)), dma((groups,)), dma((nz,)), dma((nz,)),
            dma((2, most)), dma((2, most)), dma((2, most)), dma((2, most)), dma((2,)), dma((2,)),
        ],
        compiler_params=pltpu.CompilerParams(
            collective_id=0, has_side_effects=True, vmem_limit_bytes=48 * 1024 * 1024
        ),
    )(
        tokens, out_grad, probs.T, routes.T,
        w_gate.reshape(rows_of, ff), w_up.reshape(rows_of, ff), w_down.reshape(down_rows, width),
    )


def build(mesh, nx, ny, groups, cap):
    nz = mesh.shape["expert"]

    def local(*args):
        token_grad, gate_grad, up_grad = body(nx, ny, nz, groups, cap, *args)
        return token_grad, gate_grad[None], up_grad[None]

    return jax.shard_map(
        local,
        mesh=mesh,
        in_specs=(P(("dp", "expert"), None),) * 4 + (P("expert", "dp", None),) * 3,
        out_specs=(P(("dp", "expert"), None), P("expert", "dp", None), P("expert", "dp", None)),
        check_vma=False,
    )


def solution(mesh):
    return build(mesh, 4, 4, 4, 24)
```

```python
import functools

import jax
import jax.numpy as jnp
from jax import lax
from jax.experimental import pallas as pl
from jax.experimental.pallas import tpu as pltpu
from jax.sharding import PartitionSpec as P

MESH = pl.DeviceIdType.MESH
F32 = jnp.float32
BF16 = jnp.bfloat16
NN = (((1,), (0,)), ((), ()))
NT = (((1,), (1,)), ((), ()))
TN = (((0,), (0,)), ((), ()))


def dot(a, b, dims):
    return lax.dot_general(a, b, dims, preferred_element_type=F32)


def kernel(
    nx, ny, nz, groups, cap,
    tokens_in, grad_in, probs_in, routes_in, gate_in, up_in, down_in,
    token_out, gate_out, up_out,
    tokens_ref, grad_ref, probs_ref, routes_ref, gate_ref, up_ref,
    sel, send, recv, wg, wu, wd, stage, xall, daall, dcall, own_part, sib_out, sib_in, ret, back,
    gacc, uacc, gterm, uterm, grelay1, urelay1, gbox1, ubox1, gmid, umid, grelay2, urelay2, gbox2, ubox2,
    swap_out, swap_in,
    in_sem, z_send, z_recv, f_send, f_recv, w0_send, w0_recv, w1_send, w1_recv, w2_send, w2_recv,
    p_send, p_recv, b_send, b_recv, r1_send, r1_recv, r2_send, r2_recv, r3_send, r3_recv,
):
    dp = lax.axis_index("dp")
    z = lax.axis_index("expert")
    chip = dp // 2
    core = lax.rem(dp, 2)
    x = chip // ny
    y = lax.rem(chip, ny)
    tok, width = tokens_ref.shape
    rows_of, ff = gate_ref.shape
    fh = ff // 2
    down_rows = wd.shape[2]
    quarter = down_rows // 4
    tile = ny * down_rows
    half_width = width // 2
    rows_per = 2 * cap

    sibling = (chip * 2 + (1 - core), z)

    def along_x(step):
        return ((lax.rem(x + step + nx, nx) * ny + y) * 2 + core, z)

    def along_y(step):
        return ((x * ny + lax.rem(y + step + ny, ny)) * 2 + core, z)

    def offset(pos):
        i = pos // 2
        return nz // 2 + i * (2 * lax.rem(pos, 2) - 1)

    def remote(src, dst, send_sem, recv_sem, device):
        return pltpu.make_async_remote_copy(
            src_ref=src, dst_ref=dst, send_sem=send_sem, recv_sem=recv_sem,
            device_id=device, device_id_type=MESH,
        )

    fetches = [
        pltpu.make_async_copy(src, dst, in_sem.at[i])
        for i, (src, dst) in enumerate((
            (routes_in, routes_ref), (probs_in, probs_ref), (tokens_in, tokens_ref), (grad_in, grad_ref),
            (gate_in, gate_ref), (up_in, up_ref), (down_in, wd.at[x, y]),
        ))
    ]
    for fetch in fetches:
        fetch.start()

    barrier = pltpu.get_barrier_semaphore()

    def greet(device):
        pl.semaphore_signal(barrier, inc=1, device_id=device, device_id_type=MESH)

    def sides(n):
        return {1: (), 2: (1,), 4: (1, -1)}[n]

    greet(sibling)
    for side in sides(nx):
        greet(along_x(side))
    for side in sides(ny):
        greet(along_y(side))

    def greet_z(k, carry):
        greet((dp, lax.rem(z + k, nz)))
        return carry

    lax.fori_loop(1, nz, greet_z, 0)

    for fetch in fetches[:2]:
        fetch.wait()
    experts = lax.broadcasted_iota(jnp.int32, (nz, tok), 0)
    first = routes_ref[0:1, :]
    second = routes_ref[1:2, :]
    is_first = (experts == first).astype(F32)
    is_second = (experts == second).astype(F32)
    earlier = (
        lax.broadcasted_iota(jnp.int32, (tok, tok), 0) < lax.broadcasted_iota(jnp.int32, (tok, tok), 1)
    ).astype(F32).astype(BF16)
    before = dot((is_first + is_second).astype(BF16), earlier, NN)
    place_first = first.astype(F32) * cap + jnp.sum(before * is_first, axis=0, keepdims=True)
    place_second = second.astype(F32) * cap + jnp.sum(before * is_second, axis=0, keepdims=True)
    slots = lax.broadcasted_iota(jnp.int32, (nz * cap, tok), 0).astype(F32)
    in_first = (slots == place_first).astype(F32)
    in_second = (slots == place_second).astype(F32)
    weight = jnp.sum(in_first * probs_ref[0:1, :] + in_second * probs_ref[1:2, :], axis=1, keepdims=True)
    sel[...] = (in_first + in_second).astype(BF16)
    for fetch in fetches[2:4]:
        fetch.wait()
    rows_x = dot(sel[...], tokens_ref[...], NN).reshape(nz, cap, width)
    rows_g = (dot(sel[...], grad_ref[...], NN) * weight).reshape(nz, cap, width)
    send[...] = jnp.concatenate([rows_x, rows_g], axis=1).astype(BF16)
    recv[0, 0] = send[z]

    pl.semaphore_wait(barrier, nz + len(sides(nx)) + len(sides(ny)))

    def z_copy(pos):
        other = lax.rem(z + offset(pos), nz)
        return remote(send.at[other], recv.at[0, pos], z_send.at[pos], z_recv.at[pos], (dp, other))

    def z_start(pos, carry):
        z_copy(pos).start()
        return carry

    lax.fori_loop(1, nz, z_start, 0)

    lanes = lax.broadcasted_iota(jnp.int32, (rows_of, 128), 1) < 64

    def w0(which):
        full = (wg, wu)[which]
        return remote(stage.at[which], full.at[x, y, core], w0_send.at[which], w0_recv.at[which], sibling)

    for which, (ref, full) in enumerate(((gate_ref, wg), (up_ref, wu))):
        fetches[4 + which].wait()
        for j in range(fh // 128):
            even = ref[:, 256 * j:256 * j + 128].astype(F32)
            odd = ref[:, 256 * j + 128:256 * j + 256].astype(F32)
            low = jnp.where(lanes, even, pltpu.roll(odd, 64, 1))
            high = jnp.where(lanes, pltpu.roll(even, 64, 1), odd)
            full[x, y, core, :, 128 * j:128 * j + 128] = jnp.where(core == 0, low, high).astype(BF16)
            stage[which, :, 128 * j:128 * j + 128] = jnp.where(core == 0, high, low).astype(BF16)
        w0(which).start()

    def down_part(base, h):
        return pl.ds(base, 2 * quarter) if h is None else pl.ds(base + h * quarter, quarter)

    def gate_x(i, h):
        return wg.at[i, y] if h is None else wg.at[i, y, h]

    def gate_y(j, h):
        return wg.at[:, j] if h is None else wg.at[:, j, h]

    def up_y(j, h):
        return wu.at[x, j] if h is None else wu.at[x, j, h]

    def up_x(i, h):
        return wu.at[i] if h is None else wu.at[i, :, h]

    def low_x(i, h):
        return wd.at[i, y, down_part(0, h)]

    def low_y(j, h):
        return wd.at[:, j, down_part(0, h)]

    def high_y(j, h):
        return wd.at[x, j, down_part(2 * quarter, h)]

    def high_x(i, h):
        return wd.at[i, :, down_part(2 * quarter, h)]

    def gather(n, me, piece, device, send_sem, recv_sem):
        def copy(kind):
            if kind < 2:
                ref = piece(me, None)
            else:
                ref = piece(lax.rem(me + (n - 1 if kind == 2 else 1), n), kind - 2)
            step = 1 if kind % 2 == 0 else -1
            return remote(ref, ref, send_sem.at[kind], recv_sem.at[kind], device(step))

        return tuple(copy(kind) for kind in {1: (), 2: (0,), 4: (0, 1, 2, 3)}[n])

    phase1 = [
        gather(n, me, piece, device, w1_send.at[i], w1_recv.at[i])
        for i, (n, me, piece, device) in enumerate((
            (nx, x, low_x, along_x), (ny, y, high_y, along_y), (nx, x, gate_x, along_x), (ny, y, up_y, along_y),
        ))
    ]
    phase2 = [
        gather(n, me, piece, device, w2_send.at[i], w2_recv.at[i])
        for i, (n, me, piece, device) in enumerate((
            (ny, y, low_y, along_y), (nx, x, high_x, along_x), (ny, y, gate_y, along_y), (nx, x, up_x, along_x),
        ))
    ]

    def started(copies):
        for copy in copies:
            copy.start()

    def arrived(copies):
        for copy in copies:
            copy.wait_recv()

    fetches[6].wait()
    for i in (0, 1):
        started(phase1[i][:2])
    for which in range(2):
        w0(which).wait_recv()
        started(phase1[2 + which][:2])
    for i in range(4):
        arrived(phase1[i][:2])
        started(phase1[i][2:])
    for i in range(4):
        arrived(phase1[i][2:])
        started(phase2[i][:2])

    def f_copy(pos):
        return remote(recv.at[0, pos], recv.at[1, pos], f_send.at[pos], f_recv.at[pos], sibling)

    def forward(group):
        low, high = groups[group:group + 2]

        def one(pos, carry):
            z_copy(pos).wait_recv()
            f_copy(pos).start()
            return carry

        if low == 0:
            f_copy(0).start()
        lax.fori_loop(max(low, 1), high, one, 0)

    def f_wait(group):
        def one(pos, carry):
            f_copy(pos).wait_recv()
            return carry

        lax.fori_loop(groups[group], groups[group + 1], one, 0)

    def span(group):
        low, high = groups[group:group + 2]
        return pl.ds(low * cap, (high - low) * cap), pl.ds(low * rows_per, (high - low) * rows_per)

    def p_copy(group):
        rows, _ = span(group)
        return remote(sib_out.at[rows], sib_in.at[rows], p_send.at[group], p_recv.at[group], sibling)

    def work(group):
        low, high = groups[group:group + 2]
        count = (high - low) * rows_per
        f_wait(group)
        mine, both = span(group)
        got = recv[:, low:high].astype(F32)
        gx = got[:, :, :cap].reshape(count, width).astype(BF16)
        gg = got[:, :, cap:].reshape(count, width).astype(BF16)
        xall[both] = gx

        def step(t, total):
            cols = pl.ds(pl.multiple_of(t * tile, tile), tile)
            w_g = wg[:, :, :, :, cols].reshape(width, tile)
            w_u = wu[:, :, :, :, cols].reshape(width, tile)
            w_d = wd[t].reshape(tile, width)
            a = dot(gx, w_g, NN)
            c = dot(gx, w_u, NN)
            dh = dot(gg, w_d, NT)
            s = jax.nn.sigmoid(a)
            da = (dh * c * s * (1.0 + a * (1.0 - s))).astype(BF16)
            dc = (dh * a * s).astype(BF16)
            daall[both, cols] = da
            dcall[both, cols] = dc
            return total + dot(da, w_g, NT) + dot(dc, w_u, NT)

        total = lax.fori_loop(0, fh // tile, step, jnp.zeros((count, width), F32))
        own_part[mine] = total[:count // 2]
        sib_out[mine] = total[count // 2:]
        p_copy(group).start()

    def b_copy(pos):
        other = lax.rem(z + nz - offset(pos), nz)
        return remote(ret.at[pos], back.at[z], b_send.at[pos], b_recv.at[z], (dp, other))

    def b_wait(other):
        return remote(ret.at[0], back.at[other], b_send.at[0], b_recv.at[other], (dp, other))

    def join(group):
        low, high = groups[group:group + 2]
        p_copy(group).wait_recv()
        mine, _ = span(group)
        rows = (own_part[mine] + sib_in[mine]).reshape(high - low, cap, width)
        ret[low:high] = jnp.concatenate([rows[:, :, :half_width], rows[:, :, half_width:]], axis=1).astype(BF16)
        if low == 0:
            back[z] = ret[0]

    def give_back(group):
        def one(pos, carry):
            b_copy(pos).start()
            return carry

        low, high = groups[group:group + 2]
        lax.fori_loop(max(low, 1), high, one, 0)

    block_rows = ny * 2 * rows_of
    last = len(groups) - 2
    settled = groups[last] * rows_per
    late = pl.ds(settled, nz * rows_per - settled)

    def term(ref, i, rows):
        cols = pl.ds(pl.multiple_of(i * block_rows, block_rows), block_rows)
        return dot(xall[rows, cols], ref[rows, :], TN)

    def settle(i, carry):
        rows = pl.ds(0, settled)
        gacc[i] = term(daall, i, rows)
        uacc[i] = term(dcall, i, rows)
        return carry

    for i in range(last):
        if i == 0:
            forward(0)
            for k in range(4):
                arrived(phase2[k][:2])
                started(phase2[k][2:])
            for k in range(4):
                arrived(phase2[k][2:])
        else:
            forward(i)
            join(i - 1)
        work(i)
    lax.fori_loop(0, nx, settle, 0)
    join(last - 1)
    forward(last)
    for i in range(last):
        give_back(i)
    work(last)

    def ring(n, me, block, device, relay, inbox, send_sem, recv_sem):
        def at(step):
            return lax.rem(me + step, n)

        def copy(kind):
            if kind < 2:
                src, dst = block(at(2), kind), relay.at[kind]
            elif kind < 4:
                src, dst = block(at(1 if kind == 2 else n - 1), 3 - kind), inbox.at[kind - 2, 3 - kind]
            else:
                src, dst = block(at(1 if kind == 4 else n - 1), kind - 4), inbox.at[kind - 4, kind - 4]
            step = 1 if kind % 2 == 0 else -1
            return remote(src, dst, send_sem.at[kind], recv_sem.at[kind], device(step))

        kinds = {1: (), 2: (2, 4), 4: (0, 1, 2, 3, 4, 5)}[n]

        def begin():
            for kind in kinds:
                if kind < 2:
                    copy(kind).start()

        def direct():
            for kind in kinds:
                if 2 <= kind < 4:
                    copy(kind).start()

        def relayed():
            for kind in kinds:
                if kind >= 4:
                    if n == 4:
                        copy(kind - 4).wait_recv()
                        ref = block(at(1 if kind == 4 else n - 1), kind - 4)
                        ref[...] = (ref[...].astype(F32) + relay[kind - 4].astype(F32)).astype(BF16)
                    copy(kind).start()

        def total(half):
            value = block(me, half)[...].astype(F32)
            for side in range(len(sides(n))):
                value = value + inbox[side, half].astype(F32)
            return value

        def arrive():
            for kind in kinds:
                if kind >= 2:
                    copy(kind).wait_recv()

        def drain():
            for kind in kinds:
                copy(kind).wait_send()

        return begin, direct, relayed, arrive, total, drain

    def ring_of(phase, array, n, me, block, device, relay, inbox):
        sems = ((r1_send, r1_recv), (r2_send, r2_recv))[phase]
        return ring(n, me, block, device, relay, inbox, sems[0].at[array], sems[1].at[array])

    g1 = ring_of(0, 0, nx, x, lambda i, h: gterm.at[i, :, h], along_x, grelay1, gbox1)
    u1 = ring_of(0, 1, ny, y, lambda j, h: uterm.at[:, j, h], along_y, urelay1, ubox1)
    g2 = ring_of(1, 0, ny, y, lambda j, h: gmid.at[j, h], along_y, grelay2, gbox2)
    u2 = ring_of(1, 1, nx, x, lambda i, h: umid.at[i, h], along_x, urelay2, ubox2)

    def gate_term(i):
        gterm[i] = (gacc[i] + term(daall, i, late)).reshape(ny, 2, rows_of, fh).astype(BF16)

    def up_term(i, carry):
        uterm[i] = (uacc[i] + term(dcall, i, late)).reshape(ny, 2, rows_of, fh).astype(BF16)
        return carry

    if nx == 4:
        gate_term(lax.rem(x + 2, nx))
        g1[0]()
    lax.fori_loop(0, nx, up_term, 0)
    u1[0]()
    u1[1]()

    def gate_rest(k, carry):
        gate_term(lax.rem(x + 2 * k + 1, nx))
        return carry

    lax.fori_loop(0, 2 if nx == 4 else nx - 1, gate_rest, 0)
    g1[1]()
    join(last)
    give_back(last)
    g1[2]()
    u1[2]()
    gate_term(x)
    for one, mid, two in ((g1, gmid, g2), (u1, umid, u2)):
        one[3]()
        for half in range(2):
            mid[:, half] = one[4](half).astype(BF16)
        two[0]()
        two[1]()
    for two in (g2, u2):
        two[2]()

    def r3(which):
        return remote(swap_out.at[which], swap_in.at[which], r3_send.at[which], r3_recv.at[which], sibling)

    mine = []
    for which, two in enumerate((g2, u2)):
        two[3]()
        low, high = two[4](0), two[4](1)
        mine.append(jnp.where(core == 0, low, high))
        swap_out[which] = jnp.where(core == 0, high, low).astype(BF16)
        r3(which).start()

    def back_wait(k, carry):
        b_wait(lax.rem(z + k, nz)).wait_recv()
        return carry

    lax.fori_loop(1, nz, back_wait, 0)
    came = back[...].astype(F32)
    came = jnp.concatenate([came[:, :cap], came[:, cap:]], axis=2).reshape(nz * cap, width).astype(BF16)
    token_out[...] = dot(sel[...], came, TN).astype(BF16)

    for which, out in enumerate((gate_out, up_out)):
        r3(which).wait_recv()
        theirs = swap_in[which].astype(F32)
        half0 = jnp.where(core == 0, mine[which], theirs)
        half1 = jnp.where(core == 0, theirs, mine[which])
        for j in range(fh // 128):
            h0 = half0[:, 128 * j:128 * j + 128]
            h1 = half1[:, 128 * j:128 * j + 128]
            out[:, 256 * j:256 * j + 128] = jnp.where(lanes, h0, pltpu.roll(h1, 64, 1)).astype(BF16)
            out[:, 256 * j + 128:256 * j + 256] = jnp.where(lanes, pltpu.roll(h0, 64, 1), h1).astype(BF16)

    for which in range(2):
        w0(which).wait_send()
        r3(which).wait_send()
    for copies in phase1 + phase2:
        for copy in copies:
            copy.wait_send()
    for group in range(last + 1):
        p_copy(group).wait_send()
    f_copy(0).wait_send()

    def drain(pos, carry):
        z_copy(pos).wait_send()
        f_copy(pos).wait_send()
        b_copy(pos).wait_send()
        return carry

    lax.fori_loop(1, nz, drain, 0)
    for one in (g1, u1, g2, u2):
        one[5]()


def body(nx, ny, nz, groups, cap, tokens, out_grad, probs, routes, w_gate, w_up, w_down):
    tok, width = tokens.shape
    rows_of, ff = w_gate.shape[1:]
    down_rows = w_down.shape[1]
    fh = ff // 2
    vmem = pltpu.VMEM
    dma = pltpu.SemaphoreType.DMA
    return pl.pallas_call(
        functools.partial(kernel, nx, ny, nz, groups, cap),
        out_shape=(
            jax.ShapeDtypeStruct((tok, width), BF16),
            jax.ShapeDtypeStruct((rows_of, ff), BF16),
            jax.ShapeDtypeStruct((rows_of, ff), BF16),
        ),
        in_specs=[pl.BlockSpec(memory_space=pl.ANY)] * 7,
        out_specs=(pl.BlockSpec(memory_space=pltpu.VMEM),) * 3,
        scratch_shapes=[
            vmem((tok, width), BF16),
            vmem((tok, width), BF16),
            vmem((2, tok), F32),
            vmem((2, tok), jnp.int32),
            vmem((rows_of, ff), BF16),
            vmem((rows_of, ff), BF16),
            vmem((nz * cap, tok), BF16),
            vmem((nz, 2 * cap, width), BF16),
            vmem((2, nz, 2 * cap, width), BF16),
            vmem((nx, ny, 2, rows_of, fh), BF16),
            vmem((nx, ny, 2, rows_of, fh), BF16),
            vmem((nx, ny, down_rows, width), BF16),
            vmem((2, rows_of, fh), BF16),
            vmem((2 * nz * cap, width), BF16),
            vmem((2 * nz * cap, fh), BF16),
            vmem((2 * nz * cap, fh), BF16),
            vmem((nz * cap, width), F32),
            vmem((nz * cap, width), F32),
            vmem((nz * cap, width), F32),
            vmem((nz, 2 * cap, width // 2), BF16),
            vmem((nz, 2 * cap, width // 2), BF16),
            vmem((nx, ny * 2 * rows_of, fh), F32),
            vmem((nx, ny * 2 * rows_of, fh), F32),
            vmem((nx, ny, 2, rows_of, fh), BF16),
            vmem((nx, ny, 2, rows_of, fh), BF16),
            vmem((2, ny, rows_of, fh), BF16),
            vmem((2, nx, rows_of, fh), BF16),
            vmem((2, 2, ny, rows_of, fh), BF16),
            vmem((2, 2, nx, rows_of, fh), BF16),
            vmem((ny, 2, rows_of, fh), BF16),
            vmem((nx, 2, rows_of, fh), BF16),
            vmem((2, rows_of, fh), BF16),
            vmem((2, rows_of, fh), BF16),
            vmem((2, 2, rows_of, fh), BF16),
            vmem((2, 2, rows_of, fh), BF16),
            vmem((2, rows_of, fh), BF16),
            vmem((2, rows_of, fh), BF16),
            dma((7,)),
            dma((nz,)), dma((nz,)), dma((nz,)), dma((nz,)),
            dma((2,)), dma((2,)), dma((4, 4)), dma((4, 4)), dma((4, 4)), dma((4, 4)),
            dma((len(groups),)), dma((len(groups),)), dma((nz,)), dma((nz,)),
            dma((2, 6)), dma((2, 6)), dma((2, 6)), dma((2, 6)), dma((2,)), dma((2,)),
        ],
        compiler_params=pltpu.CompilerParams(
            collective_id=0, has_side_effects=True, vmem_limit_bytes=60 * 1024 * 1024
        ),
    )(
        tokens, out_grad, probs.T, routes.T,
        w_gate.reshape(rows_of, ff), w_up.reshape(rows_of, ff), w_down.reshape(down_rows, width),
    )


def build(mesh, nx, ny, groups, cap):
    nz = mesh.shape["expert"]

    def local(*args):
        token_grad, gate_grad, up_grad = body(nx, ny, nz, groups, cap, *args)
        return token_grad, gate_grad[None], up_grad[None]

    return jax.shard_map(
        local,
        mesh=mesh,
        in_specs=(P(("dp", "expert"), None),) * 4 + (P("expert", "dp", None),) * 3,
        out_specs=(P(("dp", "expert"), None), P("expert", "dp", None), P("expert", "dp", None)),
        check_vma=False,
    )


def solution(mesh):
    return build(mesh, 4, 4, (0, 4, 8, 12, 16), 24)
```

```python
import functools

import jax
import jax.numpy as jnp
from jax import lax
from jax.experimental import pallas as pl
from jax.experimental.pallas import tpu as pltpu
from jax.sharding import PartitionSpec as P

MESH = pl.DeviceIdType.MESH
F32 = jnp.float32
BF16 = jnp.bfloat16
NN = (((1,), (0,)), ((), ()))
NT = (((1,), (1,)), ((), ()))
TN = (((0,), (0,)), ((), ()))


def dot(a, b, dims):
    return lax.dot_general(a, b, dims, preferred_element_type=F32)


def kernel(
    nx, ny, nz, groups, cap,
    tokens_in, grad_in, probs_in, routes_in, gate_in, up_in, down_in,
    token_out, gate_out, up_out,
    tokens_ref, grad_ref, probs_ref, routes_ref, gate_ref, up_ref,
    sel, send, recv, wg, wu, wd, stage, xall, daall, dcall, own_part, sib_out, sib_in, ret, back,
    gacc, uacc, gterm, uterm, grelay1, urelay1, gbox1, ubox1, gmid, umid, grelay2, urelay2, gbox2, ubox2,
    swap_in, z_relay, b_relay,
    in_sem, hop_send, hop_recv, z_send, z_recv, f_send, f_recv, w0_send, w0_recv, w1_send, w1_recv, w2_send, w2_recv,
    p_send, p_recv, b_send, b_recv, r1_send, r1_recv, r2_send, r2_recv, r3_recv,
):
    dp = lax.axis_index("dp")
    z = lax.axis_index("expert")
    chip = dp // 2
    core = lax.rem(dp, 2)
    x = chip // ny
    y = lax.rem(chip, ny)
    tok, width = tokens_ref.shape
    rows_of, ff = gate_ref.shape
    fh = ff // 2
    down_rows = wd.shape[2]
    quarter = down_rows // 4
    tile = ny * down_rows
    half_width = width // 2
    rows_per = 2 * cap

    sibling = (chip * 2 + (1 - core), z)

    def along_x(step, to=core):
        return ((lax.rem(x + step + nx, nx) * ny + y) * 2 + to, z)

    def along_y(step, to=core):
        return ((x * ny + lax.rem(y + step + ny, ny)) * 2 + to, z)

    def offset(pos):
        return nz // 2 + (pos // 2) * (2 * (pos % 2) - 1)

    def remote(src, dst, send_sem, recv_sem, device):
        return pltpu.make_async_remote_copy(
            src_ref=src, dst_ref=dst, send_sem=send_sem, recv_sem=recv_sem,
            device_id=device, device_id_type=MESH,
        )

    fetches = [
        pltpu.make_async_copy(src, dst, in_sem.at[i])
        for i, (src, dst) in enumerate((
            (routes_in, routes_ref), (probs_in, probs_ref), (tokens_in, tokens_ref), (grad_in, grad_ref),
            (gate_in, gate_ref), (up_in, up_ref), (down_in, wd.at[x, y]),
        ))
    ]
    for fetch in fetches:
        fetch.start()

    barrier = pltpu.get_barrier_semaphore()

    def greet(device):
        pl.semaphore_signal(barrier, inc=1, device_id=device, device_id_type=MESH)

    def sides(n):
        return {1: (), 2: (1,), 4: (1, -1)}[n]

    greet(sibling)
    for to in range(2):
        for side in sides(nx):
            greet(along_x(side, to))
        for side in sides(ny):
            greet(along_y(side, to))

    def greet_z(k, carry):
        greet((dp, lax.rem(z + k, nz)))
        return carry

    lax.fori_loop(1, nz, greet_z, 0)

    for fetch in fetches[:2]:
        fetch.wait()
    experts = lax.broadcasted_iota(jnp.int32, (nz, tok), 0)
    first = routes_ref[0:1, :]
    second = routes_ref[1:2, :]
    is_first = (experts == first).astype(F32)
    is_second = (experts == second).astype(F32)
    earlier = (
        lax.broadcasted_iota(jnp.int32, (tok, tok), 0) < lax.broadcasted_iota(jnp.int32, (tok, tok), 1)
    ).astype(F32).astype(BF16)
    before = dot((is_first + is_second).astype(BF16), earlier, NN)
    place_first = first.astype(F32) * cap + jnp.sum(before * is_first, axis=0, keepdims=True)
    place_second = second.astype(F32) * cap + jnp.sum(before * is_second, axis=0, keepdims=True)
    slots = lax.broadcasted_iota(jnp.int32, (cap, tok), 0)

    split = nz >= 4
    direct_from = 2 if split else 1

    def z_copy(pos):
        other = lax.rem(z + offset(pos), nz)
        return remote(send.at[pos], recv.at[0, pos], z_send.at[pos], z_recv.at[pos], (dp, other))

    def halfway(hop):
        left, right = pl.ds(0, half_width), pl.ds(half_width, half_width)
        if hop == 0:
            src, dst, step = send.at[1, :, left], recv.at[0, 1, :, left], nz // 2
        elif hop == 1:
            src, dst, step = send.at[1, :, right], z_relay, nz // 2 + 1
        else:
            src, dst, step = z_relay, recv.at[0, 1, :, right], nz - 1
        return remote(src, dst, hop_send.at[0, hop], hop_recv.at[0, hop], (dp, lax.rem(z + step, nz)))

    def halfway_back(hop):
        left, right = pl.ds(0, half_width // 2), pl.ds(half_width // 2, half_width // 2)
        if hop == 0:
            src, dst, step = ret.at[1, :, left], back.at[1, :, left], nz // 2
        elif hop == 1:
            src, dst, step = ret.at[1, :, right], b_relay, nz // 2 + 1
        else:
            src, dst, step = b_relay, back.at[1, :, right], nz - 1
        return remote(src, dst, hop_send.at[1, hop], hop_recv.at[1, hop], (dp, lax.rem(z + step, nz)))

    def z_start(pos, carry):
        z_copy(pos).start()
        return carry

    for fetch in fetches[2:4]:
        fetch.wait()
    chunk = min(4, nz)
    for begin in range(0, nz, chunk):
        in_first, in_second = [], []
        for pos in range(begin, begin + chunk):
            expert = z if pos == 0 else lax.rem(z + offset(pos), nz)
            here = (slots + expert * cap).astype(F32)
            in_first.append((here == place_first).astype(F32))
            in_second.append((here == place_second).astype(F32))
        in_first = jnp.concatenate(in_first, axis=0)
        in_second = jnp.concatenate(in_second, axis=0)
        weight = jnp.sum(in_first * probs_ref[0:1, :] + in_second * probs_ref[1:2, :], axis=1, keepdims=True)
        pick = in_first + in_second
        sel[begin:begin + chunk] = pick.reshape(chunk, cap, tok)
        pick = pick.astype(BF16)
        rows_x = dot(pick, tokens_ref[...], NN).reshape(chunk, cap, width)
        rows_g = (dot(pick, grad_ref[...], NN) * weight).reshape(chunk, cap, width)
        send[begin:begin + chunk] = jnp.concatenate([rows_x, rows_g], axis=1).astype(BF16)
        if begin == 0:
            pl.semaphore_wait(barrier, nz + 2 * len(sides(nx)) + 2 * len(sides(ny)))
            if split:
                halfway(1).start()
                halfway(0).start()
        lax.fori_loop(max(begin, direct_from), begin + chunk, z_start, 0)
    recv[0, 0] = send[0]

    lanes = lax.broadcasted_iota(jnp.int32, (rows_of, 128), 1) < 64

    def w0(which):
        full = (wg, wu)[which]
        return remote(stage.at[which], full.at[x, y, core], w0_send.at[which], w0_recv.at[which], sibling)

    for which, (ref, full) in enumerate(((gate_ref, wg), (up_ref, wu))):
        fetches[4 + which].wait()
        for j in range(fh // 128):
            even = ref[:, 256 * j:256 * j + 128].astype(F32)
            odd = ref[:, 256 * j + 128:256 * j + 256].astype(F32)
            low = jnp.where(lanes, even, pltpu.roll(odd, 64, 1))
            high = jnp.where(lanes, pltpu.roll(even, 64, 1), odd)
            full[x, y, core, :, 128 * j:128 * j + 128] = jnp.where(core == 0, low, high).astype(BF16)
            stage[which, :, 128 * j:128 * j + 128] = jnp.where(core == 0, high, low).astype(BF16)
        w0(which).start()

    def down_part(base, h):
        return pl.ds(base, 2 * quarter) if h is None else pl.ds(base + h * quarter, quarter)

    def gate_x(i, h):
        return wg.at[i, y] if h is None else wg.at[i, y, h]

    def gate_y(j, h):
        return wg.at[:, j] if h is None else wg.at[:, j, h]

    def up_y(j, h):
        return wu.at[x, j] if h is None else wu.at[x, j, h]

    def up_x(i, h):
        return wu.at[i] if h is None else wu.at[i, :, h]

    def low_x(i, h):
        return wd.at[i, y, down_part(0, h)]

    def low_y(j, h):
        return wd.at[:, j, down_part(0, h)]

    def high_y(j, h):
        return wd.at[x, j, down_part(2 * quarter, h)]

    def high_x(i, h):
        return wd.at[i, :, down_part(2 * quarter, h)]

    def gather(n, me, piece, device, send_sem, recv_sem):
        def copy(kind):
            if kind < 2:
                ref = piece(me, None)
            else:
                ref = piece(lax.rem(me + (n - 1 if kind == 2 else 1), n), kind - 2)
            step = 1 if kind % 2 == 0 else -1
            return remote(ref, ref, send_sem.at[kind], recv_sem.at[kind], device(step))

        return tuple(copy(kind) for kind in {1: (), 2: (0,), 4: (0, 1, 2, 3)}[n])

    phase1 = [
        gather(n, me, piece, device, w1_send.at[i], w1_recv.at[i])
        for i, (n, me, piece, device) in enumerate((
            (nx, x, low_x, along_x), (ny, y, high_y, along_y), (nx, x, gate_x, along_x), (ny, y, up_y, along_y),
        ))
    ]
    phase2 = [
        gather(n, me, piece, device, w2_send.at[i], w2_recv.at[i])
        for i, (n, me, piece, device) in enumerate((
            (ny, y, low_y, along_y), (nx, x, high_x, along_x), (ny, y, gate_y, along_y), (nx, x, up_x, along_x),
        ))
    ]

    def started(copies):
        for copy in copies:
            copy.start()

    def arrived(copies):
        for copy in copies:
            copy.wait_recv()

    fetches[6].wait()
    for i in (0, 1):
        started(phase1[i][:2])
    for which in range(2):
        w0(which).wait_recv()
        started(phase1[2 + which][:2])
    for i in range(4):
        arrived(phase1[i][:2])
        started(phase1[i][2:])
    if split:
        halfway(1).wait_recv()
        halfway(2).start()
    for i in range(4):
        arrived(phase1[i][2:])
        started(phase2[i][:2])

    def f_copy(pos):
        return remote(recv.at[0, pos], recv.at[1, pos], f_send.at[pos], f_recv.at[pos], sibling)

    def forward(group):
        low, high = groups[group:group + 2]

        def one(pos, carry):
            z_copy(pos).wait_recv()
            f_copy(pos).start()
            return carry

        if low == 0:
            f_copy(0).start()
            if split:
                halfway(0).wait_recv()
                halfway(2).wait_recv()
                f_copy(1).start()
        lax.fori_loop(max(low, direct_from), high, one, 0)

    def f_wait(group):
        def one(pos, carry):
            f_copy(pos).wait_recv()
            return carry

        lax.fori_loop(groups[group], groups[group + 1], one, 0)

    def span(group):
        low, high = groups[group:group + 2]
        return pl.ds(low * cap, (high - low) * cap), pl.ds(low * rows_per, (high - low) * rows_per)

    def p_copy(group):
        rows, _ = span(group)
        return remote(sib_out.at[rows], sib_in.at[rows], p_send.at[group], p_recv.at[group], sibling)

    def work(group):
        low, high = groups[group:group + 2]
        count = (high - low) * rows_per
        f_wait(group)
        mine, both = span(group)
        got = recv[:, low:high].astype(F32)
        gx = got[:, :, :cap].reshape(count, width).astype(BF16)
        gg = got[:, :, cap:].reshape(count, width).astype(BF16)
        xall[both] = gx

        def step(t, total):
            cols = pl.ds(pl.multiple_of(t * tile, tile), tile)
            w_g = wg[:, :, :, :, cols].reshape(width, tile)
            w_u = wu[:, :, :, :, cols].reshape(width, tile)
            w_d = wd[t].reshape(tile, width)
            a = dot(gx, w_g, NN)
            c = dot(gx, w_u, NN)
            dh = dot(gg, w_d, NT)
            s = jax.nn.sigmoid(a)
            da = (dh * c * s * (1.0 + a * (1.0 - s))).astype(BF16)
            dc = (dh * a * s).astype(BF16)
            daall[both, cols] = da
            dcall[both, cols] = dc
            return total + dot(da, w_g, NT) + dot(dc, w_u, NT)

        total = lax.fori_loop(0, fh // tile, step, jnp.zeros((count, width), F32))
        own_part[mine] = total[:count // 2]
        sib_out[mine] = total[count // 2:]
        p_copy(group).start()

    def b_copy(pos):
        other = lax.rem(z + nz - offset(pos), nz)
        return remote(ret.at[pos], back.at[pos], b_send.at[pos], b_recv.at[pos], (dp, other))

    def join(group):
        low, high = groups[group:group + 2]
        p_copy(group).wait_recv()
        mine, _ = span(group)
        rows = (own_part[mine] + sib_in[mine]).reshape(high - low, cap, width)
        ret[low:high] = jnp.concatenate([rows[:, :, :half_width], rows[:, :, half_width:]], axis=1).astype(BF16)
        if low == 0:
            back[0] = ret[0]

    def give_back(group):
        def one(pos, carry):
            b_copy(pos).start()
            return carry

        low, high = groups[group:group + 2]
        if low == 0 and split:
            halfway_back(1).start()
            halfway_back(0).start()
        lax.fori_loop(max(low, direct_from), high, one, 0)

    block_rows = ny * 2 * rows_of
    last = len(groups) - 2
    settled = groups[last] * rows_per
    late = pl.ds(settled, nz * rows_per - settled)

    def term(ref, i, rows):
        cols = pl.ds(pl.multiple_of(i * block_rows, block_rows), block_rows)
        return dot(xall[rows, cols], ref[rows, :], TN)

    def settle(i, carry):
        rows = pl.ds(0, settled)
        gacc[i] = term(daall, i, rows)
        uacc[i] = term(dcall, i, rows)
        return carry

    for i in range(last):
        if i == 0:
            forward(0)
            for k in range(4):
                arrived(phase2[k][:2])
                started(phase2[k][2:])
            for k in range(4):
                arrived(phase2[k][2:])
        else:
            forward(i)
            join(i - 1)
        work(i)
    lax.fori_loop(0, nx, settle, 0)
    join(last - 1)
    forward(last)
    for i in range(last):
        give_back(i)
    work(last)

    def ring(n, me, block, device, relay, inbox, send_sem, recv_sem):
        def at(step):
            return lax.rem(me + step, n)

        def copy(kind):
            if kind < 2:
                src, dst = block(at(2), kind), relay.at[kind]
            elif kind < 4:
                src, dst = block(at(1 if kind == 2 else n - 1), 3 - kind), inbox.at[kind - 2, 3 - kind]
            else:
                src, dst = block(at(1 if kind == 4 else n - 1), kind - 4), inbox.at[kind - 4, kind - 4]
            step = 1 if kind % 2 == 0 else -1
            return remote(src, dst, send_sem.at[kind], recv_sem.at[kind], device(step))

        kinds = {1: (), 2: (2, 4), 4: (0, 1, 2, 3, 4, 5)}[n]

        def begin():
            for kind in kinds:
                if kind < 2:
                    copy(kind).start()

        def direct():
            for kind in kinds:
                if 2 <= kind < 4:
                    copy(kind).start()

        def relayed():
            for kind in kinds:
                if kind >= 4:
                    if n == 4:
                        copy(kind - 4).wait_recv()
                        ref = block(at(1 if kind == 4 else n - 1), kind - 4)
                        ref[...] = (ref[...].astype(F32) + relay[kind - 4].astype(F32)).astype(BF16)
                    copy(kind).start()

        def total(half):
            value = block(me, half)[...].astype(F32)
            for side in range(len(sides(n))):
                value = value + inbox[side, half].astype(F32)
            return value

        def arrive():
            for kind in kinds:
                if kind >= 2:
                    copy(kind).wait_recv()

        def drain():
            for kind in kinds:
                copy(kind).wait_send()

        return begin, direct, relayed, arrive, total, drain

    def last_ring(n, me, mid, device, relay, inbox, sib_box, send_sem, recv_sem, sib_sem):
        def at(step):
            return lax.rem(me + step, n)

        def copy(kind):
            if kind == 6:
                return remote(mid.at[me, 1 - core], sib_box, send_sem.at[6], sib_sem, sibling)
            step = 1 if kind % 2 == 0 else -1
            if kind < 2:
                return remote(
                    mid.at[at(2), kind], relay.at[kind], send_sem.at[kind], recv_sem.at[4 + kind], device(step)
                )
            side = kind % 2
            half = 3 - kind if kind < 4 else kind - 4
            return remote(
                mid.at[at(1 if side == 0 else n - 1), half], inbox.at[side, core],
                send_sem.at[kind], recv_sem.at[2 * side + core], device(step, half),
            )

        kinds = {1: (), 2: (2, 4), 4: (0, 1, 2, 3, 4, 5)}[n] + (6,)

        def begin():
            for kind in kinds:
                if kind < 4 or kind == 6:
                    copy(kind).start()

        def relayed():
            for kind in kinds:
                if 4 <= kind < 6:
                    if n == 4:
                        copy(kind - 4).wait_recv()
                        ref = mid.at[at(1 if kind == 4 else n - 1), kind - 4]
                        ref[...] = (ref[...].astype(F32) + relay[kind - 4].astype(F32)).astype(BF16)
                    copy(kind).start()

        def arrive():
            copy(6).wait_recv()
            for side in range(len(sides(n))):
                for source in range(2):
                    remote(
                        mid.at[0, 0], inbox.at[side, source], send_sem.at[0], recv_sem.at[2 * side + source], sibling
                    ).wait_recv()

        def total(source):
            own = mid[me, core].astype(F32)
            value = jnp.where(core == source, own, sib_box[...].astype(F32))
            for side in range(len(sides(n))):
                value = value + inbox[side, source].astype(F32)
            return value

        def drain():
            for kind in kinds:
                copy(kind).wait_send()

        return begin, relayed, arrive, total, drain

    g1 = ring(nx, x, lambda i, h: gterm.at[i, :, h], along_x, grelay1, gbox1, r1_send.at[0], r1_recv.at[0])
    u1 = ring(ny, y, lambda j, h: uterm.at[:, j, h], along_y, urelay1, ubox1, r1_send.at[1], r1_recv.at[1])
    g2 = last_ring(ny, y, gmid, along_y, grelay2, gbox2, swap_in.at[0], r2_send.at[0], r2_recv.at[0], r3_recv.at[0])
    u2 = last_ring(nx, x, umid, along_x, urelay2, ubox2, swap_in.at[1], r2_send.at[1], r2_recv.at[1], r3_recv.at[1])

    def gate_term(i):
        gterm[i] = (gacc[i] + term(daall, i, late)).reshape(ny, 2, rows_of, fh).astype(BF16)

    def up_term(i, carry):
        uterm[i] = (uacc[i] + term(dcall, i, late)).reshape(ny, 2, rows_of, fh).astype(BF16)
        return carry

    if nx == 4:
        gate_term(lax.rem(x + 2, nx))
        g1[0]()
    lax.fori_loop(0, nx, up_term, 0)
    u1[0]()
    u1[1]()

    def gate_rest(k, carry):
        gate_term(lax.rem(x + 2 * k + 1, nx))
        return carry

    lax.fori_loop(0, 2 if nx == 4 else nx - 1, gate_rest, 0)
    g1[1]()
    join(last)
    give_back(last)
    if split:
        halfway_back(1).wait_recv()
        halfway_back(2).start()
    g1[2]()
    u1[2]()
    gate_term(x)
    for one, mid, two in ((g1, gmid, g2), (u1, umid, u2)):
        one[3]()
        for half in range(2):
            mid[:, half] = one[4](half).astype(BF16)
        two[0]()
    for two in (g2, u2):
        two[1]()

    def back_wait(pos, carry):
        b_copy(pos).wait_recv()
        return carry

    if split:
        halfway_back(0).wait_recv()
        halfway_back(2).wait_recv()
    lax.fori_loop(direct_from, nz, back_wait, 0)
    came = back[...].astype(F32)
    came = jnp.concatenate([came[:, :cap], came[:, cap:]], axis=2).reshape(nz * cap, width).astype(BF16)
    token_out[...] = dot(sel[...].reshape(nz * cap, tok).astype(BF16), came, TN).astype(BF16)

    for two, out in ((g2, gate_out), (u2, up_out)):
        two[2]()
        half0, half1 = two[3](0), two[3](1)
        for j in range(fh // 128):
            h0 = half0[:, 128 * j:128 * j + 128]
            h1 = half1[:, 128 * j:128 * j + 128]
            out[:, 256 * j:256 * j + 128] = jnp.where(lanes, h0, pltpu.roll(h1, 64, 1)).astype(BF16)
            out[:, 256 * j + 128:256 * j + 256] = jnp.where(lanes, pltpu.roll(h0, 64, 1), h1).astype(BF16)

    for which in range(2):
        w0(which).wait_send()
    for copies in phase1 + phase2:
        for copy in copies:
            copy.wait_send()
    for group in range(last + 1):
        p_copy(group).wait_send()
    for pos in range(direct_from):
        f_copy(pos).wait_send()
    if split:
        for hop in range(3):
            halfway(hop).wait_send()
            halfway_back(hop).wait_send()

    def drain(pos, carry):
        z_copy(pos).wait_send()
        f_copy(pos).wait_send()
        b_copy(pos).wait_send()
        return carry

    lax.fori_loop(direct_from, nz, drain, 0)
    for one in (g1, u1, g2, u2):
        one[-1]()


def body(nx, ny, nz, groups, cap, tokens, out_grad, probs, routes, w_gate, w_up, w_down):
    tok, width = tokens.shape
    rows_of, ff = w_gate.shape[1:]
    down_rows = w_down.shape[1]
    fh = ff // 2
    vmem = pltpu.VMEM
    dma = pltpu.SemaphoreType.DMA
    return pl.pallas_call(
        functools.partial(kernel, nx, ny, nz, groups, cap),
        out_shape=(
            jax.ShapeDtypeStruct((tok, width), BF16),
            jax.ShapeDtypeStruct((rows_of, ff), BF16),
            jax.ShapeDtypeStruct((rows_of, ff), BF16),
        ),
        in_specs=[pl.BlockSpec(memory_space=pl.ANY)] * 7,
        out_specs=(pl.BlockSpec(memory_space=pltpu.VMEM),) * 3,
        scratch_shapes=[
            vmem((tok, width), BF16),
            vmem((tok, width), BF16),
            vmem((2, tok), F32),
            vmem((2, tok), jnp.int32),
            vmem((rows_of, ff), BF16),
            vmem((rows_of, ff), BF16),
            vmem((nz, cap, tok), F32),
            vmem((nz, 2 * cap, width), BF16),
            vmem((2, nz, 2 * cap, width), BF16),
            vmem((nx, ny, 2, rows_of, fh), BF16),
            vmem((nx, ny, 2, rows_of, fh), BF16),
            vmem((nx, ny, down_rows, width), BF16),
            vmem((2, rows_of, fh), BF16),
            vmem((2 * nz * cap, width), BF16),
            vmem((2 * nz * cap, fh), BF16),
            vmem((2 * nz * cap, fh), BF16),
            vmem((nz * cap, width), F32),
            vmem((nz * cap, width), F32),
            vmem((nz * cap, width), F32),
            vmem((nz, 2 * cap, width // 2), BF16),
            vmem((nz, 2 * cap, width // 2), BF16),
            vmem((nx, ny * 2 * rows_of, fh), F32),
            vmem((nx, ny * 2 * rows_of, fh), F32),
            vmem((nx, ny, 2, rows_of, fh), BF16),
            vmem((nx, ny, 2, rows_of, fh), BF16),
            vmem((2, ny, rows_of, fh), BF16),
            vmem((2, nx, rows_of, fh), BF16),
            vmem((2, 2, ny, rows_of, fh), BF16),
            vmem((2, 2, nx, rows_of, fh), BF16),
            vmem((ny, 2, rows_of, fh), BF16),
            vmem((nx, 2, rows_of, fh), BF16),
            vmem((2, rows_of, fh), BF16),
            vmem((2, rows_of, fh), BF16),
            vmem((2, 2, rows_of, fh), BF16),
            vmem((2, 2, rows_of, fh), BF16),
            vmem((2, rows_of, fh), BF16),
            vmem((2 * cap, width // 2), BF16),
            vmem((2 * cap, width // 4), BF16),
            dma((7,)), dma((2, 3)), dma((2, 3)),
            dma((nz,)), dma((nz,)), dma((nz,)), dma((nz,)),
            dma((2,)), dma((2,)), dma((4, 4)), dma((4, 4)), dma((4, 4)), dma((4, 4)),
            dma((len(groups),)), dma((len(groups),)), dma((nz,)), dma((nz,)),
            dma((2, 6)), dma((2, 6)), dma((2, 7)), dma((2, 6)), dma((2,)),
        ],
        compiler_params=pltpu.CompilerParams(
            collective_id=0, has_side_effects=True, vmem_limit_bytes=60 * 1024 * 1024
        ),
    )(
        tokens, out_grad, probs.T, routes.T,
        w_gate.reshape(rows_of, ff), w_up.reshape(rows_of, ff), w_down.reshape(down_rows, width),
    )


def build(mesh, nx, ny, groups, cap):
    nz = mesh.shape["expert"]

    def local(*args):
        token_grad, gate_grad, up_grad = body(nx, ny, nz, groups, cap, *args)
        return token_grad, gate_grad[None], up_grad[None]

    return jax.shard_map(
        local,
        mesh=mesh,
        in_specs=(P(("dp", "expert"), None),) * 4 + (P("expert", "dp", None),) * 3,
        out_specs=(P(("dp", "expert"), None), P("expert", "dp", None), P("expert", "dp", None)),
        check_vma=False,
    )


def solution(mesh):
    return build(mesh, 4, 4, (0, 4, 8, 12, 16), 24)
```

```python
import functools

import jax
import jax.numpy as jnp
from jax import lax
from jax.experimental import pallas as pl
from jax.experimental.pallas import tpu as pltpu
from jax.sharding import PartitionSpec as P

MESH = pl.DeviceIdType.MESH
F32 = jnp.float32
BF16 = jnp.bfloat16
NN = (((1,), (0,)), ((), ()))
NT = (((1,), (1,)), ((), ()))
TN = (((0,), (0,)), ((), ()))


def dot(a, b, dims):
    return lax.dot_general(a, b, dims, preferred_element_type=F32)


def kernel(
    nx, ny, nz, groups, cap,
    tokens_in, grad_in, probs_in, routes_in, gate_in, up_in, down_in,
    token_out, gate_out, up_out,
    tokens_ref, grad_ref, probs_ref, routes_ref, gate_ref, up_ref,
    sel, send, recv, wg, wu, wd, stage, xall, daall, dcall, own_part, sib_out, sib_in, ret, back,
    gacc, uacc, gterm, uterm, grelay1, urelay1, gbox1, ubox1, gmid, umid, gbox2, ubox2,
    swap_in,
    in_sem, z_send, z_recv, f_send, f_recv, w0_send, w0_recv, w1_send, w1_recv, w2_send, w2_recv,
    p_send, p_recv, b_send, b_recv, r1_send, r1_recv, r2_send, r2_recv, r3_recv,
):
    dp = lax.axis_index("dp")
    z = lax.axis_index("expert")
    chip = dp // 2
    core = lax.rem(dp, 2)
    x = chip // ny
    y = lax.rem(chip, ny)
    tok, width = tokens_ref.shape
    rows_of, ff = gate_ref.shape
    fh = ff // 2
    down_rows = wd.shape[2]
    quarter = down_rows // 4
    tile = ny * down_rows
    half_width = width // 2
    rows_per = 2 * cap

    sibling = (chip * 2 + (1 - core), z)

    def along_x(step, to=core):
        return ((lax.rem(x + step + nx, nx) * ny + y) * 2 + to, z)

    def along_y(step, to=core):
        return ((x * ny + lax.rem(y + step + ny, ny)) * 2 + to, z)

    def offset(pos):
        return (pos % 2) * ((pos + 1) // 2) + (1 - pos % 2) * (nz - pos // 2)

    def remote(src, dst, send_sem, recv_sem, device):
        return pltpu.make_async_remote_copy(
            src_ref=src, dst_ref=dst, send_sem=send_sem, recv_sem=recv_sem,
            device_id=device, device_id_type=MESH,
        )

    fetches = [
        pltpu.make_async_copy(src, dst, in_sem.at[i])
        for i, (src, dst) in enumerate((
            (routes_in, routes_ref), (probs_in, probs_ref), (tokens_in, tokens_ref), (grad_in, grad_ref),
            (gate_in, gate_ref), (up_in, up_ref), (down_in, wd.at[x, y]),
        ))
    ]
    for fetch in fetches:
        fetch.start()

    barrier = pltpu.get_barrier_semaphore()

    def greet(device):
        pl.semaphore_signal(barrier, inc=1, device_id=device, device_id_type=MESH)

    def sides(n):
        return {1: (), 2: (1,), 4: (1, -1)}[n]

    greet(sibling)
    for to in range(2):
        for step in range(1, nx):
            greet(along_x(step, to))
        for step in range(1, ny):
            greet(along_y(step, to))

    def greet_z(k, carry):
        greet((dp, lax.rem(z + k, nz)))
        return carry

    lax.fori_loop(1, nz, greet_z, 0)

    for fetch in fetches[:2]:
        fetch.wait()
    experts = lax.broadcasted_iota(jnp.int32, (nz, tok), 0)
    first = routes_ref[0:1, :]
    second = routes_ref[1:2, :]
    is_first = (experts == first).astype(F32)
    is_second = (experts == second).astype(F32)
    earlier = (
        lax.broadcasted_iota(jnp.int32, (tok, tok), 0) < lax.broadcasted_iota(jnp.int32, (tok, tok), 1)
    ).astype(F32).astype(BF16)
    before = dot((is_first + is_second).astype(BF16), earlier, NN)
    place_first = first.astype(F32) * cap + jnp.sum(before * is_first, axis=0, keepdims=True)
    place_second = second.astype(F32) * cap + jnp.sum(before * is_second, axis=0, keepdims=True)
    slots = lax.broadcasted_iota(jnp.int32, (cap, tok), 0)

    def z_copy(pos):
        other = lax.rem(z + offset(pos), nz)
        return remote(send.at[pos], recv.at[0, pos], z_send.at[pos], z_recv.at[pos], (dp, other))

    def z_start(pos, carry):
        z_copy(pos).start()
        return carry

    for fetch in fetches[2:4]:
        fetch.wait()
    chunk = min(4, nz)
    for begin in range(0, nz, chunk):
        in_first, in_second = [], []
        for pos in range(begin, begin + chunk):
            expert = lax.rem(z + offset(pos), nz)
            here = (slots + expert * cap).astype(F32)
            in_first.append((here == place_first).astype(F32))
            in_second.append((here == place_second).astype(F32))
        in_first = jnp.concatenate(in_first, axis=0)
        in_second = jnp.concatenate(in_second, axis=0)
        weight = jnp.sum(in_first * probs_ref[0:1, :] + in_second * probs_ref[1:2, :], axis=1, keepdims=True)
        pick = in_first + in_second
        sel[begin:begin + chunk] = pick.reshape(chunk, cap, tok)
        pick = pick.astype(BF16)
        rows_x = dot(pick, tokens_ref[...], NN).reshape(chunk, cap, width)
        rows_g = (dot(pick, grad_ref[...], NN) * weight).reshape(chunk, cap, width)
        send[begin:begin + chunk] = jnp.concatenate([rows_x, rows_g], axis=1).astype(BF16)
        if begin == 0:
            pl.semaphore_wait(barrier, nz + 2 * (nx - 1) + 2 * (ny - 1))
        lax.fori_loop(max(begin, 1), begin + chunk, z_start, 0)
    recv[0, 0] = send[0]

    lanes = lax.broadcasted_iota(jnp.int32, (rows_of, 128), 1) < 64

    def w0(which):
        full = (wg, wu)[which]
        return remote(stage.at[which], full.at[x, y, core], w0_send.at[which], w0_recv.at[which], sibling)

    for which, (ref, full) in enumerate(((gate_ref, wg), (up_ref, wu))):
        fetches[4 + which].wait()
        for j in range(fh // 128):
            even = ref[:, 256 * j:256 * j + 128].astype(F32)
            odd = ref[:, 256 * j + 128:256 * j + 256].astype(F32)
            low = jnp.where(lanes, even, pltpu.roll(odd, 64, 1))
            high = jnp.where(lanes, pltpu.roll(even, 64, 1), odd)
            full[x, y, core, :, 128 * j:128 * j + 128] = jnp.where(core == 0, low, high).astype(BF16)
            stage[which, :, 128 * j:128 * j + 128] = jnp.where(core == 0, high, low).astype(BF16)
        w0(which).start()

    def down_part(base, h):
        return pl.ds(base, 2 * quarter) if h is None else pl.ds(base + h * quarter, quarter)

    def gate_x(i, h):
        return wg.at[i, y] if h is None else wg.at[i, y, h]

    def gate_y(j, h):
        return wg.at[:, j] if h is None else wg.at[:, j, h]

    def up_y(j, h):
        return wu.at[x, j] if h is None else wu.at[x, j, h]

    def up_x(i, h):
        return wu.at[i] if h is None else wu.at[i, :, h]

    def low_x(i, h):
        return wd.at[i, y, down_part(0, h)]

    def low_y(j, h):
        return wd.at[:, j, down_part(0, h)]

    def high_y(j, h):
        return wd.at[x, j, down_part(2 * quarter, h)]

    def high_x(i, h):
        return wd.at[i, :, down_part(2 * quarter, h)]

    def gather(n, me, piece, device, send_sem, recv_sem):
        def copy(kind):
            if kind < 2:
                ref = piece(me, None)
            else:
                ref = piece(lax.rem(me + (n - 1 if kind == 2 else 1), n), kind - 2)
            step = 1 if kind % 2 == 0 else -1
            return remote(ref, ref, send_sem.at[kind], recv_sem.at[kind], device(step))

        return tuple(copy(kind) for kind in {1: (), 2: (0,), 4: (0, 1, 2, 3)}[n])

    phase1 = [
        gather(n, me, piece, device, w1_send.at[i], w1_recv.at[i])
        for i, (n, me, piece, device) in enumerate((
            (nx, x, low_x, along_x), (ny, y, high_y, along_y), (nx, x, gate_x, along_x), (ny, y, up_y, along_y),
        ))
    ]
    phase2 = [
        gather(n, me, piece, device, w2_send.at[i], w2_recv.at[i])
        for i, (n, me, piece, device) in enumerate((
            (ny, y, low_y, along_y), (nx, x, high_x, along_x), (ny, y, gate_y, along_y), (nx, x, up_x, along_x),
        ))
    ]

    def started(copies):
        for copy in copies:
            copy.start()

    def arrived(copies):
        for copy in copies:
            copy.wait_recv()

    fetches[6].wait()
    for i in (0, 1):
        started(phase1[i][:2])
    for which in range(2):
        w0(which).wait_recv()
        started(phase1[2 + which][:2])
    for i in range(4):
        arrived(phase1[i][:2])
        started(phase1[i][2:])
    for i in range(4):
        arrived(phase1[i][2:])
        started(phase2[i][:2])

    def f_copy(pos):
        return remote(recv.at[0, pos], recv.at[1, pos], f_send.at[pos], f_recv.at[pos], sibling)

    def forward(group):
        low, high = groups[group:group + 2]

        def one(pos, carry):
            z_copy(pos).wait_recv()
            f_copy(pos).start()
            return carry

        if low == 0:
            f_copy(0).start()
        lax.fori_loop(max(low, 1), high, one, 0)

    def f_wait(group):
        def one(pos, carry):
            f_copy(pos).wait_recv()
            return carry

        lax.fori_loop(groups[group], groups[group + 1], one, 0)

    def span(group):
        low, high = groups[group:group + 2]
        return pl.ds(low * cap, (high - low) * cap), pl.ds(low * rows_per, (high - low) * rows_per)

    def p_copy(group):
        rows, _ = span(group)
        return remote(sib_out.at[rows], sib_in.at[rows], p_send.at[group], p_recv.at[group], sibling)

    def work(group, whole):
        low, high = groups[group:group + 2]
        count = (high - low) * rows_per
        f_wait(group)
        _, both = span(group)
        got = recv[:, low:high].astype(F32)
        gx = got[:, :, :cap].reshape(count, width).astype(BF16)
        gg = got[:, :, cap:].reshape(count, width).astype(BF16)
        xall[both] = gx

        def step(t, total):
            cols = pl.ds(pl.multiple_of(t * tile, tile), tile)
            w_g = wg[:, :, :, :, cols].reshape(width, tile)
            w_u = wu[:, :, :, :, cols].reshape(width, tile)
            w_d = wd[t].reshape(tile, width)
            a = dot(gx, w_g, NN)
            c = dot(gx, w_u, NN)
            dh = dot(gg, w_d, NT)
            s = jax.nn.sigmoid(a)
            da = (dh * c * s * (1.0 + a * (1.0 - s))).astype(BF16)
            dc = (dh * a * s).astype(BF16)
            daall[both, cols] = da
            dcall[both, cols] = dc
            return total + dot(da, w_g, NT) + dot(dc, w_u, NT) if whole else total

        if whole:
            hand_over(group, lax.fori_loop(0, fh // tile, step, jnp.zeros((count, width), F32)))
        else:
            lax.fori_loop(0, fh // tile, step, 0)

    def row_part(group):
        low, high = groups[group:group + 2]
        _, both = span(group)

        def step(t, total):
            cols = pl.ds(pl.multiple_of(t * tile, tile), tile)
            w_g = wg[:, :, :, :, cols].reshape(width, tile)
            w_u = wu[:, :, :, :, cols].reshape(width, tile)
            return total + dot(daall[both, cols], w_g, NT) + dot(dcall[both, cols], w_u, NT)

        zero = jnp.zeros(((high - low) * rows_per, width), F32)
        hand_over(group, lax.fori_loop(0, fh // tile, step, zero))

    def hand_over(group, total):
        mine, _ = span(group)
        count = total.shape[0]
        own_part[mine] = total[:count // 2]
        sib_out[mine] = total[count // 2:]
        p_copy(group).start()

    def b_copy(pos):
        other = lax.rem(z + nz - offset(pos), nz)
        return remote(ret.at[pos], back.at[pos], b_send.at[pos], b_recv.at[pos], (dp, other))

    def join(group):
        low, high = groups[group:group + 2]
        p_copy(group).wait_recv()
        mine, _ = span(group)
        rows = (own_part[mine] + sib_in[mine]).reshape(high - low, cap, width)
        ret[low:high] = jnp.concatenate([rows[:, :, :half_width], rows[:, :, half_width:]], axis=1).astype(BF16)
        if low == 0:
            back[0] = ret[0]

    def give_back(group):
        def one(pos, carry):
            b_copy(pos).start()
            return carry

        low, high = groups[group:group + 2]
        lax.fori_loop(max(low, 1), high, one, 0)

    block_rows = ny * 2 * rows_of
    last = len(groups) - 2
    settled = groups[last] * rows_per
    late = pl.ds(settled, nz * rows_per - settled)

    def term(ref, i, rows):
        cols = pl.ds(pl.multiple_of(i * block_rows, block_rows), block_rows)
        return dot(xall[rows, cols], ref[rows, :], TN)

    def settle(i, carry):
        rows = pl.ds(0, settled)
        gacc[i] = term(daall, i, rows)
        uacc[i] = term(dcall, i, rows)
        return carry

    forward(0)
    for k in range(4):
        arrived(phase2[k][:2])
        started(phase2[k][2:])
    for k in range(4):
        arrived(phase2[k][2:])
    for i in range(last):
        if i > 0:
            forward(i)
            join(i - 1)
        work(i, True)
    lax.fori_loop(0, nx, settle, 0)
    join(last - 1)
    forward(last)
    for i in range(last):
        give_back(i)
    work(last, False)

    def ring(n, me, block, device, relay, inbox, send_sem, recv_sem):
        def at(step):
            return lax.rem(me + step, n)

        def copy(kind):
            if kind < 2:
                src, dst = block(at(2), kind), relay.at[kind]
            elif kind < 4:
                src, dst = block(at(1 if kind == 2 else n - 1), 3 - kind), inbox.at[kind - 2, 3 - kind]
            else:
                src, dst = block(at(1 if kind == 4 else n - 1), kind - 4), inbox.at[kind - 4, kind - 4]
            step = 1 if kind % 2 == 0 else -1
            return remote(src, dst, send_sem.at[kind], recv_sem.at[kind], device(step))

        kinds = {1: (), 2: (2, 4), 4: (0, 1, 2, 3, 4, 5)}[n]

        def begin():
            for kind in kinds:
                if kind < 2:
                    copy(kind).start()

        def direct():
            for kind in kinds:
                if 2 <= kind < 4:
                    copy(kind).start()

        def relayed():
            for kind in kinds:
                if kind >= 4:
                    if n == 4:
                        copy(kind - 4).wait_recv()
                        ref = block(at(1 if kind == 4 else n - 1), kind - 4)
                        ref[...] = (ref[...].astype(F32) + relay[kind - 4].astype(F32)).astype(BF16)
                    copy(kind).start()

        def total(half):
            value = block(me, half)[...].astype(F32)
            for side in range(len(sides(n))):
                value = value + inbox[side, half].astype(F32)
            return value

        def arrive():
            for kind in kinds:
                if kind >= 2:
                    copy(kind).wait_recv()

        def drain():
            for kind in kinds:
                copy(kind).wait_send()

        return begin, direct, relayed, arrive, total, drain

    def last_sum(n, me, mid, device, inbox, sib_box, send_sem, recv_sem, sib_sem):
        def copy(step, half):
            return remote(
                mid.at[lax.rem(me + step, n), half], inbox.at[step, core],
                send_sem.at[2 * step + half], recv_sem.at[2 * step + core], device(step, half),
            )

        across = remote(mid.at[me, 1 - core], sib_box, send_sem.at[0], sib_sem, sibling)
        steps = {1: (), 2: (1,), 4: (2, 1, 3)}[n]

        def begin():
            for step in steps:
                for half in range(2):
                    copy(step, half).start()
            across.start()

        def arrive():
            across.wait_recv()
            for step in steps:
                for source in range(2):
                    remote(
                        mid.at[0, 0], inbox.at[step, source], send_sem.at[1],
                        recv_sem.at[2 * step + source], sibling,
                    ).wait_recv()

        def total(source):
            own = mid[me, core].astype(F32)
            value = jnp.where(core == source, own, sib_box[...].astype(F32))
            for step in steps:
                value = value + inbox[step, source].astype(F32)
            return value

        def drain():
            across.wait_send()
            for step in steps:
                for half in range(2):
                    copy(step, half).wait_send()

        return begin, arrive, total, drain

    g1 = ring(nx, x, lambda i, h: gterm.at[i, :, h], along_x, grelay1, gbox1, r1_send.at[0], r1_recv.at[0])
    u1 = ring(ny, y, lambda j, h: uterm.at[:, j, h], along_y, urelay1, ubox1, r1_send.at[1], r1_recv.at[1])
    g2 = last_sum(ny, y, gmid, along_y, gbox2, swap_in.at[0], r2_send.at[0], r2_recv.at[0], r3_recv.at[0])
    u2 = last_sum(nx, x, umid, along_x, ubox2, swap_in.at[1], r2_send.at[1], r2_recv.at[1], r3_recv.at[1])

    def gate_term(i):
        gterm[i] = (gacc[i] + term(daall, i, late)).reshape(ny, 2, rows_of, fh).astype(BF16)

    def up_term(i, carry):
        uterm[i] = (uacc[i] + term(dcall, i, late)).reshape(ny, 2, rows_of, fh).astype(BF16)
        return carry

    if nx == 4:
        gate_term(lax.rem(x + 2, nx))
        g1[0]()
    lax.fori_loop(0, nx, up_term, 0)
    u1[0]()
    u1[1]()
    row_part(last)

    def gate_rest(k, carry):
        gate_term(lax.rem(x + 2 * k + 1, nx))
        return carry

    lax.fori_loop(0, 2 if nx == 4 else nx - 1, gate_rest, 0)
    g1[1]()
    join(last)
    give_back(last)
    g1[2]()
    u1[2]()
    gate_term(x)
    for one, mid, two in ((g1, gmid, g2), (u1, umid, u2)):
        one[3]()
        for half in range(2):
            mid[:, half] = one[4](half).astype(BF16)
        two[0]()

    def back_wait(pos, carry):
        b_copy(pos).wait_recv()
        return carry

    lax.fori_loop(1, nz, back_wait, 0)
    came = back[...].astype(F32)
    came = jnp.concatenate([came[:, :cap], came[:, cap:]], axis=2).reshape(nz * cap, width).astype(BF16)
    token_out[...] = dot(sel[...].reshape(nz * cap, tok).astype(BF16), came, TN).astype(BF16)

    for two, out in ((g2, gate_out), (u2, up_out)):
        two[1]()
        half0, half1 = two[2](0), two[2](1)
        for j in range(fh // 128):
            h0 = half0[:, 128 * j:128 * j + 128]
            h1 = half1[:, 128 * j:128 * j + 128]
            out[:, 256 * j:256 * j + 128] = jnp.where(lanes, h0, pltpu.roll(h1, 64, 1)).astype(BF16)
            out[:, 256 * j + 128:256 * j + 256] = jnp.where(lanes, pltpu.roll(h0, 64, 1), h1).astype(BF16)

    for which in range(2):
        w0(which).wait_send()
    for copies in phase1 + phase2:
        for copy in copies:
            copy.wait_send()
    for group in range(last + 1):
        p_copy(group).wait_send()
    f_copy(0).wait_send()

    def drain(pos, carry):
        z_copy(pos).wait_send()
        f_copy(pos).wait_send()
        b_copy(pos).wait_send()
        return carry

    lax.fori_loop(1, nz, drain, 0)
    for one in (g1, u1, g2, u2):
        one[-1]()


def body(nx, ny, nz, groups, cap, tokens, out_grad, probs, routes, w_gate, w_up, w_down):
    tok, width = tokens.shape
    rows_of, ff = w_gate.shape[1:]
    down_rows = w_down.shape[1]
    fh = ff // 2
    vmem = pltpu.VMEM
    dma = pltpu.SemaphoreType.DMA
    return pl.pallas_call(
        functools.partial(kernel, nx, ny, nz, groups, cap),
        out_shape=(
            jax.ShapeDtypeStruct((tok, width), BF16),
            jax.ShapeDtypeStruct((rows_of, ff), BF16),
            jax.ShapeDtypeStruct((rows_of, ff), BF16),
        ),
        in_specs=[pl.BlockSpec(memory_space=pl.ANY)] * 7,
        out_specs=(pl.BlockSpec(memory_space=pltpu.VMEM),) * 3,
        scratch_shapes=[
            vmem((tok, width), BF16),
            vmem((tok, width), BF16),
            vmem((2, tok), F32),
            vmem((2, tok), jnp.int32),
            vmem((rows_of, ff), BF16),
            vmem((rows_of, ff), BF16),
            vmem((nz, cap, tok), F32),
            vmem((nz, 2 * cap, width), BF16),
            vmem((2, nz, 2 * cap, width), BF16),
            vmem((nx, ny, 2, rows_of, fh), BF16),
            vmem((nx, ny, 2, rows_of, fh), BF16),
            vmem((nx, ny, down_rows, width), BF16),
            vmem((2, rows_of, fh), BF16),
            vmem((2 * nz * cap, width), BF16),
            vmem((2 * nz * cap, fh), BF16),
            vmem((2 * nz * cap, fh), BF16),
            vmem((nz * cap, width), F32),
            vmem((nz * cap, width), F32),
            vmem((nz * cap, width), F32),
            vmem((nz, 2 * cap, width // 2), BF16),
            vmem((nz, 2 * cap, width // 2), BF16),
            vmem((nx, ny * 2 * rows_of, fh), F32),
            vmem((nx, ny * 2 * rows_of, fh), F32),
            vmem((nx, ny, 2, rows_of, fh), BF16),
            vmem((nx, ny, 2, rows_of, fh), BF16),
            vmem((2, ny, rows_of, fh), BF16),
            vmem((2, nx, rows_of, fh), BF16),
            vmem((2, 2, ny, rows_of, fh), BF16),
            vmem((2, 2, nx, rows_of, fh), BF16),
            vmem((ny, 2, rows_of, fh), BF16),
            vmem((nx, 2, rows_of, fh), BF16),
            vmem((4, 2, rows_of, fh), BF16),
            vmem((4, 2, rows_of, fh), BF16),
            vmem((2, rows_of, fh), BF16),
            dma((7,)),
            dma((nz,)), dma((nz,)), dma((nz,)), dma((nz,)),
            dma((2,)), dma((2,)), dma((4, 4)), dma((4, 4)), dma((4, 4)), dma((4, 4)),
            dma((len(groups),)), dma((len(groups),)), dma((nz,)), dma((nz,)),
            dma((2, 6)), dma((2, 6)), dma((2, 8)), dma((2, 8)), dma((2,)),
        ],
        compiler_params=pltpu.CompilerParams(
            collective_id=0, has_side_effects=True, vmem_limit_bytes=60 * 1024 * 1024
        ),
    )(
        tokens, out_grad, probs.T, routes.T,
        w_gate.reshape(rows_of, ff), w_up.reshape(rows_of, ff), w_down.reshape(down_rows, width),
    )


def build(mesh, nx, ny, groups, cap):
    nz = mesh.shape["expert"]

    def local(*args):
        token_grad, gate_grad, up_grad = body(nx, ny, nz, groups, cap, *args)
        return token_grad, gate_grad[None], up_grad[None]

    return jax.shard_map(
        local,
        mesh=mesh,
        in_specs=(P(("dp", "expert"), None),) * 4 + (P("expert", "dp", None),) * 3,
        out_specs=(P(("dp", "expert"), None), P("expert", "dp", None), P("expert", "dp", None)),
        check_vma=False,
    )


def solution(mesh):
    return build(mesh, 4, 4, (0, 4, 8, 12, 16), 24)
```

```python
import functools

import jax
import jax.numpy as jnp
from jax import lax
from jax.experimental import pallas as pl
from jax.experimental.pallas import tpu as pltpu
from jax.sharding import PartitionSpec as P

MESH = pl.DeviceIdType.MESH
F32 = jnp.float32
BF16 = jnp.bfloat16
NN = (((1,), (0,)), ((), ()))
NT = (((1,), (1,)), ((), ()))
TN = (((0,), (0,)), ((), ()))


def dot(a, b, dims):
    return lax.dot_general(a, b, dims, preferred_element_type=F32)


def kernel(
    nx, ny, nz, groups, cap,
    tokens_in, grad_in, probs_in, routes_in, gate_in, up_in, down_in,
    token_out, gate_out, up_out,
    tokens_ref, grad_ref, probs_ref, routes_ref, gate_ref, up_ref,
    sel, send, recv, wg, wu, wd, stage, xall, daall, dcall, own_part, sib_out, sib_in, ret, back,
    gacc, uacc, gterm, uterm, grelay1, urelay1, gbox1, ubox1, gmid, umid, gbox2, ubox2,
    swap_in,
    in_sem, z_send, z_recv, f_send, f_recv, w0_send, w0_recv, w1_send, w1_recv, w2_send, w2_recv,
    p_send, p_recv, b_send, b_recv, r1_send, r1_recv, r2_send, r2_recv, r3_recv,
):
    dp = lax.axis_index("dp")
    z = lax.axis_index("expert")
    chip = dp // 2
    core = lax.rem(dp, 2)
    x = chip // ny
    y = lax.rem(chip, ny)
    tok, width = tokens_ref.shape
    rows_of, ff = gate_ref.shape
    fh = ff // 2
    down_rows = wd.shape[2]
    quarter = down_rows // 4
    tile = ny * down_rows
    half_width = width // 2
    rows_per = 2 * cap

    sibling = (chip * 2 + (1 - core), z)

    def along_x(step, to=core):
        return ((lax.rem(x + step + nx, nx) * ny + y) * 2 + to, z)

    def along_y(step, to=core):
        return ((x * ny + lax.rem(y + step + ny, ny)) * 2 + to, z)

    def offset(pos):
        return (pos % 2) * ((pos + 1) // 2) + (1 - pos % 2) * (nz - pos // 2)

    def remote(src, dst, send_sem, recv_sem, device):
        return pltpu.make_async_remote_copy(
            src_ref=src, dst_ref=dst, send_sem=send_sem, recv_sem=recv_sem,
            device_id=device, device_id_type=MESH,
        )

    fetches = [
        pltpu.make_async_copy(src, dst, in_sem.at[i])
        for i, (src, dst) in enumerate((
            (routes_in, routes_ref), (probs_in, probs_ref), (tokens_in, tokens_ref), (grad_in, grad_ref),
            (gate_in, gate_ref), (up_in, up_ref), (down_in, wd.at[x, y]),
        ))
    ]
    for fetch in fetches:
        fetch.start()

    barrier = pltpu.get_barrier_semaphore()

    def greet(device):
        pl.semaphore_signal(barrier, inc=1, device_id=device, device_id_type=MESH)

    def sides(n):
        return {1: (), 2: (1,), 4: (1, -1)}[n]

    greet(sibling)
    for to in range(2):
        for step in range(1, nx):
            greet(along_x(step, to))
        for step in range(1, ny):
            greet(along_y(step, to))

    def greet_z(k, carry):
        greet((dp, lax.rem(z + k, nz)))
        return carry

    lax.fori_loop(1, nz, greet_z, 0)

    lanes = lax.broadcasted_iota(jnp.int32, (rows_of, 128), 1) < 64

    def w0(which):
        full = (wg, wu)[which]
        return remote(stage.at[which], full.at[x, y, core], w0_send.at[which], w0_recv.at[which], sibling)

    for which, (ref, full) in enumerate(((gate_ref, wg), (up_ref, wu))):
        fetches[4 + which].wait()
        for j in range(fh // 128):
            even = ref[:, 256 * j:256 * j + 128].astype(F32)
            odd = ref[:, 256 * j + 128:256 * j + 256].astype(F32)
            low = jnp.where(lanes, even, pltpu.roll(odd, 64, 1))
            high = jnp.where(lanes, pltpu.roll(even, 64, 1), odd)
            full[x, y, core, :, 128 * j:128 * j + 128] = jnp.where(core == 0, low, high).astype(BF16)
            stage[which, :, 128 * j:128 * j + 128] = jnp.where(core == 0, high, low).astype(BF16)

    def down_part(base, h):
        return pl.ds(base, 2 * quarter) if h is None else pl.ds(base + h * quarter, quarter)

    def gate_x(i, h):
        return wg.at[i, y] if h is None else wg.at[i, y, h]

    def gate_y(j, h):
        return wg.at[:, j] if h is None else wg.at[:, j, h]

    def up_y(j, h):
        return wu.at[x, j] if h is None else wu.at[x, j, h]

    def up_x(i, h):
        return wu.at[i] if h is None else wu.at[i, :, h]

    def low_x(i, h):
        return wd.at[i, y, down_part(0, h)]

    def low_y(j, h):
        return wd.at[:, j, down_part(0, h)]

    def high_y(j, h):
        return wd.at[x, j, down_part(2 * quarter, h)]

    def high_x(i, h):
        return wd.at[i, :, down_part(2 * quarter, h)]

    def gather(n, me, piece, device, send_sem, recv_sem):
        def copy(kind):
            if kind < 2:
                ref = piece(me, None)
            else:
                ref = piece(lax.rem(me + (n - 1 if kind == 2 else 1), n), kind - 2)
            step = 1 if kind % 2 == 0 else -1
            return remote(ref, ref, send_sem.at[kind], recv_sem.at[kind], device(step))

        return tuple(copy(kind) for kind in {1: (), 2: (0,), 4: (0, 1, 2, 3)}[n])

    phase1 = [
        gather(n, me, piece, device, w1_send.at[i], w1_recv.at[i])
        for i, (n, me, piece, device) in enumerate((
            (nx, x, low_x, along_x), (ny, y, high_y, along_y), (nx, x, gate_x, along_x), (ny, y, up_y, along_y),
        ))
    ]
    phase2 = [
        gather(n, me, piece, device, w2_send.at[i], w2_recv.at[i])
        for i, (n, me, piece, device) in enumerate((
            (ny, y, low_y, along_y), (nx, x, high_x, along_x), (ny, y, gate_y, along_y), (nx, x, up_x, along_x),
        ))
    ]

    def started(copies):
        for copy in copies:
            copy.start()

    def arrived(copies):
        for copy in copies:
            copy.wait_recv()

    for fetch in fetches[:2]:
        fetch.wait()
    experts = lax.broadcasted_iota(jnp.int32, (nz, tok), 0)
    first = routes_ref[0:1, :]
    second = routes_ref[1:2, :]
    is_first = (experts == first).astype(F32)
    is_second = (experts == second).astype(F32)
    earlier = (
        lax.broadcasted_iota(jnp.int32, (tok, tok), 0) < lax.broadcasted_iota(jnp.int32, (tok, tok), 1)
    ).astype(F32).astype(BF16)
    before = dot((is_first + is_second).astype(BF16), earlier, NN)
    place_first = first.astype(F32) * cap + jnp.sum(before * is_first, axis=0, keepdims=True)
    place_second = second.astype(F32) * cap + jnp.sum(before * is_second, axis=0, keepdims=True)
    slots = lax.broadcasted_iota(jnp.int32, (cap, tok), 0)

    def z_copy(pos):
        other = lax.rem(z + offset(pos), nz)
        return remote(send.at[pos], recv.at[0, pos], z_send.at[pos], z_recv.at[pos], (dp, other))

    def z_start(pos, carry):
        z_copy(pos).start()
        return carry

    for fetch in fetches[2:4]:
        fetch.wait()
    chunk = min(4, nz)
    for begin in range(0, nz, chunk):
        in_first, in_second = [], []
        for pos in range(begin, begin + chunk):
            expert = lax.rem(z + offset(pos), nz)
            here = (slots + expert * cap).astype(F32)
            in_first.append((here == place_first).astype(F32))
            in_second.append((here == place_second).astype(F32))
        in_first = jnp.concatenate(in_first, axis=0)
        in_second = jnp.concatenate(in_second, axis=0)
        weight = jnp.sum(in_first * probs_ref[0:1, :] + in_second * probs_ref[1:2, :], axis=1, keepdims=True)
        pick = in_first + in_second
        sel[begin:begin + chunk] = pick.reshape(chunk, cap, tok)
        pick = pick.astype(BF16)
        rows_x = dot(pick, tokens_ref[...], NN).reshape(chunk, cap, width)
        rows_g = (dot(pick, grad_ref[...], NN) * weight).reshape(chunk, cap, width)
        send[begin:begin + chunk] = jnp.concatenate([rows_x, rows_g], axis=1).astype(BF16)
        if begin == 0:
            pl.semaphore_wait(barrier, nz + 2 * (nx - 1) + 2 * (ny - 1))
            for which in range(2):
                w0(which).start()
            fetches[6].wait()
            for i in (0, 1):
                started(phase1[i][:2])
        lax.fori_loop(max(begin, 1), begin + chunk, z_start, 0)
    recv[0, 0] = send[0]

    for which in range(2):
        w0(which).wait_recv()
        started(phase1[2 + which][:2])
    for i in range(4):
        arrived(phase1[i][:2])
        started(phase1[i][2:])
    for i in range(4):
        arrived(phase1[i][2:])
        started(phase2[i][:2])

    def f_copy(pos):
        return remote(recv.at[0, pos], recv.at[1, pos], f_send.at[pos], f_recv.at[pos], sibling)

    def forward(group):
        low, high = groups[group:group + 2]

        def one(pos, carry):
            z_copy(pos).wait_recv()
            f_copy(pos).start()
            return carry

        if low == 0:
            f_copy(0).start()
        lax.fori_loop(max(low, 1), high, one, 0)

    def f_wait(group):
        def one(pos, carry):
            f_copy(pos).wait_recv()
            return carry

        lax.fori_loop(groups[group], groups[group + 1], one, 0)

    def span(group):
        low, high = groups[group:group + 2]
        return pl.ds(low * cap, (high - low) * cap), pl.ds(low * rows_per, (high - low) * rows_per)

    def p_copy(group):
        rows, _ = span(group)
        return remote(sib_out.at[rows], sib_in.at[rows], p_send.at[group], p_recv.at[group], sibling)

    def work(group, whole):
        low, high = groups[group:group + 2]
        count = (high - low) * rows_per
        f_wait(group)
        _, both = span(group)
        got = recv[:, low:high].astype(F32)
        gx = got[:, :, :cap].reshape(count, width).astype(BF16)
        gg = got[:, :, cap:].reshape(count, width).astype(BF16)
        xall[both] = gx

        def step(t, total):
            cols = pl.ds(pl.multiple_of(t * tile, tile), tile)
            w_g = wg[:, :, :, :, cols].reshape(width, tile)
            w_u = wu[:, :, :, :, cols].reshape(width, tile)
            w_d = wd[t].reshape(tile, width)
            a = dot(gx, w_g, NN)
            c = dot(gx, w_u, NN)
            dh = dot(gg, w_d, NT)
            s = jax.nn.sigmoid(a)
            da = (dh * c * s * (1.0 + a * (1.0 - s))).astype(BF16)
            dc = (dh * a * s).astype(BF16)
            daall[both, cols] = da
            dcall[both, cols] = dc
            return total + dot(da, w_g, NT) + dot(dc, w_u, NT) if whole else total

        if whole:
            hand_over(group, lax.fori_loop(0, fh // tile, step, jnp.zeros((count, width), F32)))
        else:
            lax.fori_loop(0, fh // tile, step, 0)

    def row_part(group):
        low, high = groups[group:group + 2]
        _, both = span(group)

        def step(t, total):
            cols = pl.ds(pl.multiple_of(t * tile, tile), tile)
            w_g = wg[:, :, :, :, cols].reshape(width, tile)
            w_u = wu[:, :, :, :, cols].reshape(width, tile)
            return total + dot(daall[both, cols], w_g, NT) + dot(dcall[both, cols], w_u, NT)

        zero = jnp.zeros(((high - low) * rows_per, width), F32)
        hand_over(group, lax.fori_loop(0, fh // tile, step, zero))

    def hand_over(group, total):
        mine, _ = span(group)
        count = total.shape[0]
        own_part[mine] = total[:count // 2]
        sib_out[mine] = total[count // 2:]
        p_copy(group).start()

    def b_copy(pos):
        other = lax.rem(z + nz - offset(pos), nz)
        return remote(ret.at[pos], back.at[pos], b_send.at[pos], b_recv.at[pos], (dp, other))

    def join(group):
        low, high = groups[group:group + 2]
        p_copy(group).wait_recv()
        mine, _ = span(group)
        rows = (own_part[mine] + sib_in[mine]).reshape(high - low, cap, width)
        ret[low:high] = jnp.concatenate([rows[:, :, :half_width], rows[:, :, half_width:]], axis=1).astype(BF16)
        if low == 0:
            back[0] = ret[0]

    def give_back(group):
        def one(pos, carry):
            b_copy(pos).start()
            return carry

        low, high = groups[group:group + 2]
        lax.fori_loop(max(low, 1), high, one, 0)

    block_rows = ny * 2 * rows_of
    last = len(groups) - 2
    settled = groups[last] * rows_per
    late = pl.ds(settled, nz * rows_per - settled)

    def term(ref, i, rows):
        cols = pl.ds(pl.multiple_of(i * block_rows, block_rows), block_rows)
        return dot(xall[rows, cols], ref[rows, :], TN)

    def settle(i, carry):
        rows = pl.ds(0, settled)
        gacc[i] = term(daall, i, rows)
        uacc[i] = term(dcall, i, rows)
        return carry

    forward(0)
    for k in range(4):
        arrived(phase2[k][:2])
        started(phase2[k][2:])
    for k in range(4):
        arrived(phase2[k][2:])
    for i in range(last):
        if i > 0:
            forward(i)
            join(i - 1)
        work(i, True)
    lax.fori_loop(0, nx, settle, 0)
    join(last - 1)
    forward(last)
    for i in range(last):
        give_back(i)
    work(last, False)

    def ring(n, me, block, device, relay, inbox, send_sem, recv_sem):
        def at(step):
            return lax.rem(me + step, n)

        def copy(kind):
            if kind < 2:
                src, dst = block(at(2), kind), relay.at[kind]
            elif kind < 4:
                src, dst = block(at(1 if kind == 2 else n - 1), 3 - kind), inbox.at[kind - 2, 3 - kind]
            else:
                src, dst = block(at(1 if kind == 4 else n - 1), kind - 4), inbox.at[kind - 4, kind - 4]
            step = 1 if kind % 2 == 0 else -1
            return remote(src, dst, send_sem.at[kind], recv_sem.at[kind], device(step))

        kinds = {1: (), 2: (2, 4), 4: (0, 1, 2, 3, 4, 5)}[n]

        def begin():
            for kind in kinds:
                if kind < 2:
                    copy(kind).start()

        def direct():
            for kind in kinds:
                if 2 <= kind < 4:
                    copy(kind).start()

        def relayed():
            for kind in kinds:
                if kind >= 4:
                    if n == 4:
                        copy(kind - 4).wait_recv()
                        ref = block(at(1 if kind == 4 else n - 1), kind - 4)
                        ref[...] = (ref[...].astype(F32) + relay[kind - 4].astype(F32)).astype(BF16)
                    copy(kind).start()

        def total(half):
            value = block(me, half)[...].astype(F32)
            for side in range(len(sides(n))):
                value = value + inbox[side, half].astype(F32)
            return value

        def arrive():
            for kind in kinds:
                if kind >= 2:
                    copy(kind).wait_recv()

        def drain():
            for kind in kinds:
                copy(kind).wait_send()

        return begin, direct, relayed, arrive, total, drain

    def last_sum(n, me, mid, device, inbox, sib_box, send_sem, recv_sem, sib_sem):
        def copy(step, half):
            return remote(
                mid.at[lax.rem(me + step, n), half], inbox.at[step, core],
                send_sem.at[2 * step + half], recv_sem.at[2 * step + core], device(step, half),
            )

        across = remote(mid.at[me, 1 - core], sib_box, send_sem.at[0], sib_sem, sibling)
        steps = {1: (), 2: (1,), 4: (2, 1, 3)}[n]

        def begin():
            for step in steps:
                for half in range(2):
                    copy(step, half).start()
            across.start()

        def arrive():
            across.wait_recv()
            for step in steps:
                for source in range(2):
                    remote(
                        mid.at[0, 0], inbox.at[step, source], send_sem.at[1],
                        recv_sem.at[2 * step + source], sibling,
                    ).wait_recv()

        def total(source):
            own = mid[me, core].astype(F32)
            value = jnp.where(core == source, own, sib_box[...].astype(F32))
            for step in steps:
                value = value + inbox[step, source].astype(F32)
            return value

        def drain():
            across.wait_send()
            for step in steps:
                for half in range(2):
                    copy(step, half).wait_send()

        return begin, arrive, total, drain

    g1 = ring(nx, x, lambda i, h: gterm.at[i, :, h], along_x, grelay1, gbox1, r1_send.at[0], r1_recv.at[0])
    u1 = ring(ny, y, lambda j, h: uterm.at[:, j, h], along_y, urelay1, ubox1, r1_send.at[1], r1_recv.at[1])
    g2 = last_sum(ny, y, gmid, along_y, gbox2, swap_in.at[0], r2_send.at[0], r2_recv.at[0], r3_recv.at[0])
    u2 = last_sum(nx, x, umid, along_x, ubox2, swap_in.at[1], r2_send.at[1], r2_recv.at[1], r3_recv.at[1])

    def gate_term(i):
        gterm[i] = (gacc[i] + term(daall, i, late)).reshape(ny, 2, rows_of, fh).astype(BF16)

    def up_term(i, carry):
        uterm[i] = (uacc[i] + term(dcall, i, late)).reshape(ny, 2, rows_of, fh).astype(BF16)
        return carry

    if nx == 4:
        gate_term(lax.rem(x + 2, nx))
        g1[0]()
    lax.fori_loop(0, nx, up_term, 0)
    u1[0]()
    u1[1]()
    row_part(last)

    def gate_rest(k, carry):
        gate_term(lax.rem(x + 2 * k + 1, nx))
        return carry

    lax.fori_loop(0, 2 if nx == 4 else nx - 1, gate_rest, 0)
    g1[1]()
    join(last)
    give_back(last)
    g1[2]()
    u1[2]()
    gate_term(x)
    for one, mid, two in ((g1, gmid, g2), (u1, umid, u2)):
        one[3]()
        for half in range(2):
            mid[:, half] = one[4](half).astype(BF16)
        two[0]()

    def back_wait(pos, carry):
        b_copy(pos).wait_recv()
        return carry

    lax.fori_loop(1, nz, back_wait, 0)
    came = back[...].astype(F32)
    came = jnp.concatenate([came[:, :cap], came[:, cap:]], axis=2).reshape(nz * cap, width).astype(BF16)
    token_out[...] = dot(sel[...].reshape(nz * cap, tok).astype(BF16), came, TN)

    for two, out in ((g2, gate_out), (u2, up_out)):
        two[1]()
        half0, half1 = two[2](0), two[2](1)
        for j in range(fh // 128):
            h0 = half0[:, 128 * j:128 * j + 128]
            h1 = half1[:, 128 * j:128 * j + 128]
            out[:, 256 * j:256 * j + 128] = jnp.where(lanes, h0, pltpu.roll(h1, 64, 1))
            out[:, 256 * j + 128:256 * j + 256] = jnp.where(lanes, pltpu.roll(h0, 64, 1), h1)

    for which in range(2):
        w0(which).wait_send()
    for copies in phase1 + phase2:
        for copy in copies:
            copy.wait_send()
    for group in range(last + 1):
        p_copy(group).wait_send()
    f_copy(0).wait_send()

    def drain(pos, carry):
        z_copy(pos).wait_send()
        f_copy(pos).wait_send()
        b_copy(pos).wait_send()
        return carry

    lax.fori_loop(1, nz, drain, 0)
    for one in (g1, u1, g2, u2):
        one[-1]()


def body(nx, ny, nz, groups, cap, tokens, out_grad, probs, routes, w_gate, w_up, w_down):
    tok, width = tokens.shape
    rows_of, ff = w_gate.shape[1:]
    down_rows = w_down.shape[1]
    fh = ff // 2
    vmem = pltpu.VMEM
    dma = pltpu.SemaphoreType.DMA
    return pl.pallas_call(
        functools.partial(kernel, nx, ny, nz, groups, cap),
        out_shape=(
            jax.ShapeDtypeStruct((tok, width), F32),
            jax.ShapeDtypeStruct((rows_of, ff), F32),
            jax.ShapeDtypeStruct((rows_of, ff), F32),
        ),
        in_specs=[pl.BlockSpec(memory_space=pl.ANY)] * 7,
        out_specs=(pl.BlockSpec(memory_space=pltpu.VMEM),) * 3,
        scratch_shapes=[
            vmem((tok, width), BF16),
            vmem((tok, width), BF16),
            vmem((2, tok), F32),
            vmem((2, tok), jnp.int32),
            vmem((rows_of, ff), BF16),
            vmem((rows_of, ff), BF16),
            vmem((nz, cap, tok), F32),
            vmem((nz, 2 * cap, width), BF16),
            vmem((2, nz, 2 * cap, width), BF16),
            vmem((nx, ny, 2, rows_of, fh), BF16),
            vmem((nx, ny, 2, rows_of, fh), BF16),
            vmem((nx, ny, down_rows, width), BF16),
            vmem((2, rows_of, fh), BF16),
            vmem((2 * nz * cap, width), BF16),
            vmem((2 * nz * cap, fh), BF16),
            vmem((2 * nz * cap, fh), BF16),
            vmem((nz * cap, width), F32),
            vmem((nz * cap, width), F32),
            vmem((nz * cap, width), F32),
            vmem((nz, 2 * cap, width // 2), BF16),
            vmem((nz, 2 * cap, width // 2), BF16),
            vmem((nx, ny * 2 * rows_of, fh), F32),
            vmem((nx, ny * 2 * rows_of, fh), F32),
            vmem((nx, ny, 2, rows_of, fh), BF16),
            vmem((nx, ny, 2, rows_of, fh), BF16),
            vmem((2, ny, rows_of, fh), BF16),
            vmem((2, nx, rows_of, fh), BF16),
            vmem((2, 2, ny, rows_of, fh), BF16),
            vmem((2, 2, nx, rows_of, fh), BF16),
            vmem((ny, 2, rows_of, fh), BF16),
            vmem((nx, 2, rows_of, fh), BF16),
            vmem((4, 2, rows_of, fh), BF16),
            vmem((4, 2, rows_of, fh), BF16),
            vmem((2, rows_of, fh), BF16),
            dma((7,)),
            dma((nz,)), dma((nz,)), dma((nz,)), dma((nz,)),
            dma((2,)), dma((2,)), dma((4, 4)), dma((4, 4)), dma((4, 4)), dma((4, 4)),
            dma((len(groups),)), dma((len(groups),)), dma((nz,)), dma((nz,)),
            dma((2, 6)), dma((2, 6)), dma((2, 8)), dma((2, 8)), dma((2,)),
        ],
        compiler_params=pltpu.CompilerParams(
            collective_id=0, has_side_effects=True, vmem_limit_bytes=60 * 1024 * 1024
        ),
    )(
        tokens, out_grad, probs.T, routes.T,
        w_gate.reshape(rows_of, ff), w_up.reshape(rows_of, ff), w_down.reshape(down_rows, width),
    )


def build(mesh, nx, ny, groups, cap):
    nz = mesh.shape["expert"]

    def local(*args):
        token_grad, gate_grad, up_grad = body(nx, ny, nz, groups, cap, *args)
        return token_grad.astype(BF16), gate_grad[None].astype(BF16), up_grad[None].astype(BF16)

    return jax.shard_map(
        local,
        mesh=mesh,
        in_specs=(P(("dp", "expert"), None),) * 4 + (P("expert", "dp", None),) * 3,
        out_specs=(P(("dp", "expert"), None), P("expert", "dp", None), P("expert", "dp", None)),
        check_vma=False,
    )


def solution(mesh):
    return build(mesh, 4, 4, (0, 4, 8, 12, 16), 24)
```

```python
import functools

import jax
import jax.numpy as jnp
from jax import lax
from jax.experimental import pallas as pl
from jax.experimental.pallas import tpu as pltpu
from jax.sharding import PartitionSpec as P

MESH = pl.DeviceIdType.MESH
F32 = jnp.float32
BF16 = jnp.bfloat16
NN = (((1,), (0,)), ((), ()))
NT = (((1,), (1,)), ((), ()))
TN = (((0,), (0,)), ((), ()))


def dot(a, b, dims):
    return lax.dot_general(a, b, dims, preferred_element_type=F32)


def kernel(
    nx, ny, nz, groups, cap,
    tokens_in, grad_in, probs_in, routes_in, gate_in, up_in, down_in,
    token_out, gate_out, up_out,
    tokens_ref, grad_ref, probs_ref, routes_ref, gate_ref, up_ref,
    sel, send, recv, wg, wu, wd, stage, xall, daall, dcall, own_part, sib_out, sib_in, ret, back,
    gterm, uterm, grelay1, urelay1, gbox1, ubox1, gmid, umid, gbox2, ubox2,
    swap_in,
    in_sem, z_send, z_recv, f_send, f_recv, w0_send, w0_recv, w1_send, w1_recv, w2_send, w2_recv,
    p_send, p_recv, b_send, b_recv, r1_send, r1_recv, r2_send, r2_recv, r3_recv,
):
    dp = lax.axis_index("dp")
    z = lax.axis_index("expert")
    chip = dp // 2
    core = lax.rem(dp, 2)
    x = chip // ny
    y = lax.rem(chip, ny)
    tok, width = tokens_ref.shape
    rows_of, ff = gate_ref.shape
    fh = ff // 2
    down_rows = wd.shape[2]
    quarter = down_rows // 4
    tile = ny * down_rows
    half_width = width // 2
    rows_per = 2 * cap

    sibling = (chip * 2 + (1 - core), z)

    def along_x(step, to=core):
        return ((lax.rem(x + step + nx, nx) * ny + y) * 2 + to, z)

    def along_y(step, to=core):
        return ((x * ny + lax.rem(y + step + ny, ny)) * 2 + to, z)

    def offset(pos):
        return (pos % 2) * ((pos + 1) // 2) + (1 - pos % 2) * (nz - pos // 2)

    def remote(src, dst, send_sem, recv_sem, device):
        return pltpu.make_async_remote_copy(
            src_ref=src, dst_ref=dst, send_sem=send_sem, recv_sem=recv_sem,
            device_id=device, device_id_type=MESH,
        )

    fetches = [
        pltpu.make_async_copy(src, dst, in_sem.at[i])
        for i, (src, dst) in enumerate((
            (routes_in, routes_ref), (probs_in, probs_ref), (tokens_in, tokens_ref), (grad_in, grad_ref),
            (gate_in, gate_ref), (up_in, up_ref), (down_in, wd.at[x, y]),
        ))
    ]
    for fetch in fetches:
        fetch.start()

    barrier = pltpu.get_barrier_semaphore()

    def greet(device):
        pl.semaphore_signal(barrier, inc=1, device_id=device, device_id_type=MESH)

    def sides(n):
        return {1: (), 2: (1,), 4: (1, -1)}[n]

    greet(sibling)
    for to in range(2):
        for step in range(1, nx):
            greet(along_x(step, to))
        for step in range(1, ny):
            greet(along_y(step, to))

    def greet_z(k, carry):
        greet((dp, lax.rem(z + k, nz)))
        return carry

    lax.fori_loop(1, nz, greet_z, 0)

    lanes = lax.broadcasted_iota(jnp.int32, (rows_of, 128), 1) < 64

    def w0(which):
        full = (wg, wu)[which]
        return remote(stage.at[which], full.at[x, y, core], w0_send.at[which], w0_recv.at[which], sibling)

    for which, (ref, full) in enumerate(((gate_ref, wg), (up_ref, wu))):
        fetches[4 + which].wait()
        for j in range(fh // 128):
            even = ref[:, 256 * j:256 * j + 128].astype(F32)
            odd = ref[:, 256 * j + 128:256 * j + 256].astype(F32)
            low = jnp.where(lanes, even, pltpu.roll(odd, 64, 1))
            high = jnp.where(lanes, pltpu.roll(even, 64, 1), odd)
            full[x, y, core, :, 128 * j:128 * j + 128] = jnp.where(core == 0, low, high).astype(BF16)
            stage[which, :, 128 * j:128 * j + 128] = jnp.where(core == 0, high, low).astype(BF16)

    def down_part(base, h):
        return pl.ds(base, 2 * quarter) if h is None else pl.ds(base + h * quarter, quarter)

    def gate_x(i, h):
        return wg.at[i, y] if h is None else wg.at[i, y, h]

    def gate_y(j, h):
        return wg.at[:, j] if h is None else wg.at[:, j, h]

    def up_y(j, h):
        return wu.at[x, j] if h is None else wu.at[x, j, h]

    def up_x(i, h):
        return wu.at[i] if h is None else wu.at[i, :, h]

    def low_x(i, h):
        return wd.at[i, y, down_part(0, h)]

    def low_y(j, h):
        return wd.at[:, j, down_part(0, h)]

    def high_y(j, h):
        return wd.at[x, j, down_part(2 * quarter, h)]

    def high_x(i, h):
        return wd.at[i, :, down_part(2 * quarter, h)]

    def gather(n, me, piece, device, send_sem, recv_sem):
        def copy(kind):
            if kind < 2:
                ref = piece(me, None)
            else:
                ref = piece(lax.rem(me + (n - 1 if kind == 2 else 1), n), kind - 2)
            step = 1 if kind % 2 == 0 else -1
            return remote(ref, ref, send_sem.at[kind], recv_sem.at[kind], device(step))

        return tuple(copy(kind) for kind in {1: (), 2: (0,), 4: (0, 1, 2, 3)}[n])

    phase1 = [
        gather(n, me, piece, device, w1_send.at[i], w1_recv.at[i])
        for i, (n, me, piece, device) in enumerate((
            (nx, x, low_x, along_x), (ny, y, high_y, along_y), (nx, x, gate_x, along_x), (ny, y, up_y, along_y),
        ))
    ]
    phase2 = [
        gather(n, me, piece, device, w2_send.at[i], w2_recv.at[i])
        for i, (n, me, piece, device) in enumerate((
            (ny, y, low_y, along_y), (nx, x, high_x, along_x), (ny, y, gate_y, along_y), (nx, x, up_x, along_x),
        ))
    ]

    def started(copies):
        for copy in copies:
            copy.start()

    def arrived(copies):
        for copy in copies:
            copy.wait_recv()

    for fetch in fetches[:2]:
        fetch.wait()
    experts = lax.broadcasted_iota(jnp.int32, (nz, tok), 0)
    first = routes_ref[0:1, :]
    second = routes_ref[1:2, :]
    is_first = (experts == first).astype(F32)
    is_second = (experts == second).astype(F32)
    earlier = (
        lax.broadcasted_iota(jnp.int32, (tok, tok), 0) < lax.broadcasted_iota(jnp.int32, (tok, tok), 1)
    ).astype(F32).astype(BF16)
    before = dot((is_first + is_second).astype(BF16), earlier, NN)
    place_first = first.astype(F32) * cap + jnp.sum(before * is_first, axis=0, keepdims=True)
    place_second = second.astype(F32) * cap + jnp.sum(before * is_second, axis=0, keepdims=True)
    slots = lax.broadcasted_iota(jnp.int32, (cap, tok), 0)

    def z_copy(pos):
        other = lax.rem(z + offset(pos), nz)
        return remote(send.at[pos], recv.at[0, pos], z_send.at[pos], z_recv.at[pos], (dp, other))

    def z_start(pos, carry):
        z_copy(pos).start()
        return carry

    for fetch in fetches[2:4]:
        fetch.wait()
    chunk = min(4, nz)
    for begin in range(0, nz, chunk):
        in_first, in_second = [], []
        for pos in range(begin, begin + chunk):
            expert = lax.rem(z + offset(pos), nz)
            here = (slots + expert * cap).astype(F32)
            in_first.append((here == place_first).astype(F32))
            in_second.append((here == place_second).astype(F32))
        in_first = jnp.concatenate(in_first, axis=0)
        in_second = jnp.concatenate(in_second, axis=0)
        weight = jnp.sum(in_first * probs_ref[0:1, :] + in_second * probs_ref[1:2, :], axis=1, keepdims=True)
        pick = in_first + in_second
        sel[begin:begin + chunk] = pick.reshape(chunk, cap, tok)
        pick = pick.astype(BF16)
        rows_x = dot(pick, tokens_ref[...], NN).reshape(chunk, cap, width)
        rows_g = (dot(pick, grad_ref[...], NN) * weight).reshape(chunk, cap, width)
        send[begin:begin + chunk] = jnp.concatenate([rows_x, rows_g], axis=1).astype(BF16)
        if begin == 0:
            pl.semaphore_wait(barrier, nz + 2 * (nx - 1) + 2 * (ny - 1))
            for which in range(2):
                w0(which).start()
            fetches[6].wait()
            for i in (0, 1):
                started(phase1[i][:2])
        lax.fori_loop(max(begin, 1), begin + chunk, z_start, 0)
    recv[0, 0] = send[0]

    for which in range(2):
        w0(which).wait_recv()
        started(phase1[2 + which][:2])
    for i in range(4):
        arrived(phase1[i][:2])
        started(phase1[i][2:])
    for i in range(4):
        arrived(phase1[i][2:])
        started(phase2[i][:2])

    def f_copy(pos):
        return remote(recv.at[0, pos], recv.at[1, pos], f_send.at[pos], f_recv.at[pos], sibling)

    def forward(group):
        low, high = groups[group:group + 2]

        def one(pos, carry):
            z_copy(pos).wait_recv()
            f_copy(pos).start()
            return carry

        if low == 0:
            f_copy(0).start()
        lax.fori_loop(max(low, 1), high, one, 0)

    def f_wait(group):
        def one(pos, carry):
            f_copy(pos).wait_recv()
            return carry

        lax.fori_loop(groups[group], groups[group + 1], one, 0)

    def span(group):
        low, high = groups[group:group + 2]
        return pl.ds(low * cap, (high - low) * cap), pl.ds(low * rows_per, (high - low) * rows_per)

    def p_copy(group):
        rows, _ = span(group)
        return remote(sib_out.at[rows], sib_in.at[rows], p_send.at[group], p_recv.at[group], sibling)

    def work(group, whole):
        low, high = groups[group:group + 2]
        count = (high - low) * rows_per
        f_wait(group)
        _, both = span(group)
        got = recv[:, low:high].astype(F32)
        gx = got[:, :, :cap].reshape(count, width).astype(BF16)
        gg = got[:, :, cap:].reshape(count, width).astype(BF16)
        xall[both] = gx

        def step(t, total):
            cols = pl.ds(pl.multiple_of(t * tile, tile), tile)
            w_g = wg[:, :, :, :, cols].reshape(width, tile)
            w_u = wu[:, :, :, :, cols].reshape(width, tile)
            w_d = wd[t].reshape(tile, width)
            a = dot(gx, w_g, NN)
            c = dot(gx, w_u, NN)
            dh = dot(gg, w_d, NT)
            s = jax.nn.sigmoid(a)
            da = (dh * c * s * (1.0 + a * (1.0 - s))).astype(BF16)
            dc = (dh * a * s).astype(BF16)
            daall[both, cols] = da
            dcall[both, cols] = dc
            return total + dot(da, w_g, NT) + dot(dc, w_u, NT) if whole else total

        if whole:
            hand_over(group, lax.fori_loop(0, fh // tile, step, jnp.zeros((count, width), F32)))
        else:
            lax.fori_loop(0, fh // tile, step, 0)

    def row_part(group):
        low, high = groups[group:group + 2]
        _, both = span(group)

        def step(t, total):
            cols = pl.ds(pl.multiple_of(t * tile, tile), tile)
            w_g = wg[:, :, :, :, cols].reshape(width, tile)
            w_u = wu[:, :, :, :, cols].reshape(width, tile)
            return total + dot(daall[both, cols], w_g, NT) + dot(dcall[both, cols], w_u, NT)

        zero = jnp.zeros(((high - low) * rows_per, width), F32)
        hand_over(group, lax.fori_loop(0, fh // tile, step, zero))

    def hand_over(group, total):
        mine, _ = span(group)
        count = total.shape[0]
        own_part[mine] = total[:count // 2]
        sib_out[mine] = total[count // 2:]
        p_copy(group).start()

    def b_copy(pos):
        other = lax.rem(z + nz - offset(pos), nz)
        return remote(ret.at[pos], back.at[pos], b_send.at[pos], b_recv.at[pos], (dp, other))

    def join(group):
        low, high = groups[group:group + 2]
        p_copy(group).wait_recv()
        mine, _ = span(group)
        rows = (own_part[mine] + sib_in[mine]).reshape(high - low, cap, width)
        ret[low:high] = jnp.concatenate([rows[:, :, :half_width], rows[:, :, half_width:]], axis=1).astype(BF16)
        if low == 0:
            back[0] = ret[0]

    def give_back(group):
        def one(pos, carry):
            b_copy(pos).start()
            return carry

        low, high = groups[group:group + 2]
        lax.fori_loop(max(low, 1), high, one, 0)

    block_rows = ny * 2 * rows_of
    last = len(groups) - 2
    def term(ref, i):
        cols = pl.ds(pl.multiple_of(i * block_rows, block_rows), block_rows)
        return dot(xall[:, cols], ref[...], TN)

    forward(0)
    for k in range(4):
        arrived(phase2[k][:2])
        started(phase2[k][2:])
    for k in range(4):
        arrived(phase2[k][2:])
    for i in range(last):
        if i > 0:
            forward(i)
            join(i - 1)
        work(i, True)
    forward(last)
    for i in range(last - 1):
        give_back(i)
    join(last - 1)
    give_back(last - 1)
    work(last, False)

    def ring(n, me, block, device, relay, inbox, send_sem, recv_sem):
        def at(step):
            return lax.rem(me + step, n)

        def copy(kind):
            if kind < 2:
                src, dst = block(at(2), kind), relay.at[kind]
            elif kind < 4:
                src, dst = block(at(1 if kind == 2 else n - 1), 3 - kind), inbox.at[kind - 2, 3 - kind]
            else:
                src, dst = block(at(1 if kind == 4 else n - 1), kind - 4), inbox.at[kind - 4, kind - 4]
            step = 1 if kind % 2 == 0 else -1
            return remote(src, dst, send_sem.at[kind], recv_sem.at[kind], device(step))

        kinds = {1: (), 2: (2, 4), 4: (0, 1, 2, 3, 4, 5)}[n]

        def begin():
            for kind in kinds:
                if kind < 2:
                    copy(kind).start()

        def direct():
            for kind in kinds:
                if 2 <= kind < 4:
                    copy(kind).start()

        def relayed():
            for kind in kinds:
                if kind >= 4:
                    if n == 4:
                        copy(kind - 4).wait_recv()
                        ref = block(at(1 if kind == 4 else n - 1), kind - 4)
                        ref[...] = (ref[...].astype(F32) + relay[kind - 4].astype(F32)).astype(BF16)
                    copy(kind).start()

        def total(half):
            value = block(me, half)[...].astype(F32)
            for side in range(len(sides(n))):
                value = value + inbox[side, half].astype(F32)
            return value

        def arrive():
            for kind in kinds:
                if kind >= 2:
                    copy(kind).wait_recv()

        def drain():
            for kind in kinds:
                copy(kind).wait_send()

        return begin, direct, relayed, arrive, total, drain

    def last_sum(n, me, mid, device, inbox, sib_box, send_sem, recv_sem, sib_sem):
        def copy(step, half):
            return remote(
                mid.at[lax.rem(me + step, n), half], inbox.at[step, core],
                send_sem.at[2 * step + half], recv_sem.at[2 * step + core], device(step, half),
            )

        across = remote(mid.at[me, 1 - core], sib_box, send_sem.at[0], sib_sem, sibling)
        steps = {1: (), 2: (1,), 4: (2, 1, 3)}[n]

        def begin():
            for step in steps:
                for half in range(2):
                    copy(step, half).start()
            across.start()

        def arrive():
            across.wait_recv()
            for step in steps:
                for source in range(2):
                    remote(
                        mid.at[0, 0], inbox.at[step, source], send_sem.at[1],
                        recv_sem.at[2 * step + source], sibling,
                    ).wait_recv()

        def total(source):
            own = mid[me, core].astype(F32)
            value = jnp.where(core == source, own, sib_box[...].astype(F32))
            for step in steps:
                value = value + inbox[step, source].astype(F32)
            return value

        def drain():
            across.wait_send()
            for step in steps:
                for half in range(2):
                    copy(step, half).wait_send()

        return begin, arrive, total, drain

    g1 = ring(nx, x, lambda i, h: gterm.at[i, :, h], along_x, grelay1, gbox1, r1_send.at[0], r1_recv.at[0])
    u1 = ring(ny, y, lambda j, h: uterm.at[:, j, h], along_y, urelay1, ubox1, r1_send.at[1], r1_recv.at[1])
    g2 = last_sum(ny, y, gmid, along_y, gbox2, swap_in.at[0], r2_send.at[0], r2_recv.at[0], r3_recv.at[0])
    u2 = last_sum(nx, x, umid, along_x, ubox2, swap_in.at[1], r2_send.at[1], r2_recv.at[1], r3_recv.at[1])

    def gate_term(i):
        gterm[i] = term(daall, i).reshape(ny, 2, rows_of, fh).astype(BF16)

    def up_term(i, carry):
        uterm[i] = term(dcall, i).reshape(ny, 2, rows_of, fh).astype(BF16)
        return carry

    if nx == 4:
        gate_term(lax.rem(x + 2, nx))
        g1[0]()
    lax.fori_loop(0, nx, up_term, 0)
    u1[0]()
    u1[1]()
    row_part(last)

    def gate_rest(k, carry):
        gate_term(lax.rem(x + 2 * k + 1, nx))
        return carry

    lax.fori_loop(0, 2 if nx == 4 else nx - 1, gate_rest, 0)
    g1[1]()
    join(last)
    give_back(last)
    g1[2]()
    u1[2]()
    gate_term(x)
    for one, mid, two in ((g1, gmid, g2), (u1, umid, u2)):
        one[3]()
        for half in range(2):
            mid[:, half] = one[4](half).astype(BF16)
        two[0]()

    def back_wait(pos, carry):
        b_copy(pos).wait_recv()
        return carry

    lax.fori_loop(1, nz, back_wait, 0)
    came = back[...].astype(F32)
    came = jnp.concatenate([came[:, :cap], came[:, cap:]], axis=2).reshape(nz * cap, width).astype(BF16)
    token_out[...] = dot(sel[...].reshape(nz * cap, tok).astype(BF16), came, TN)

    for two, out in ((g2, gate_out), (u2, up_out)):
        two[1]()
        half0, half1 = two[2](0), two[2](1)
        for j in range(fh // 128):
            h0 = half0[:, 128 * j:128 * j + 128]
            h1 = half1[:, 128 * j:128 * j + 128]
            out[:, 256 * j:256 * j + 128] = jnp.where(lanes, h0, pltpu.roll(h1, 64, 1))
            out[:, 256 * j + 128:256 * j + 256] = jnp.where(lanes, pltpu.roll(h0, 64, 1), h1)

    for which in range(2):
        w0(which).wait_send()
    for copies in phase1 + phase2:
        for copy in copies:
            copy.wait_send()
    for group in range(last + 1):
        p_copy(group).wait_send()
    f_copy(0).wait_send()

    def drain(pos, carry):
        z_copy(pos).wait_send()
        f_copy(pos).wait_send()
        b_copy(pos).wait_send()
        return carry

    lax.fori_loop(1, nz, drain, 0)
    for one in (g1, u1, g2, u2):
        one[-1]()


def body(nx, ny, nz, groups, cap, tokens, out_grad, probs, routes, w_gate, w_up, w_down):
    tok, width = tokens.shape
    rows_of, ff = w_gate.shape[1:]
    down_rows = w_down.shape[1]
    fh = ff // 2
    vmem = pltpu.VMEM
    dma = pltpu.SemaphoreType.DMA
    return pl.pallas_call(
        functools.partial(kernel, nx, ny, nz, groups, cap),
        out_shape=(
            jax.ShapeDtypeStruct((tok, width), F32),
            jax.ShapeDtypeStruct((rows_of, ff), F32),
            jax.ShapeDtypeStruct((rows_of, ff), F32),
        ),
        in_specs=[pl.BlockSpec(memory_space=pl.ANY)] * 7,
        out_specs=(pl.BlockSpec(memory_space=pltpu.VMEM),) * 3,
        scratch_shapes=[
            vmem((tok, width), BF16),
            vmem((tok, width), BF16),
            vmem((2, tok), F32),
            vmem((2, tok), jnp.int32),
            vmem((rows_of, ff), BF16),
            vmem((rows_of, ff), BF16),
            vmem((nz, cap, tok), F32),
            vmem((nz, 2 * cap, width), BF16),
            vmem((2, nz, 2 * cap, width), BF16),
            vmem((nx, ny, 2, rows_of, fh), BF16),
            vmem((nx, ny, 2, rows_of, fh), BF16),
            vmem((nx, ny, down_rows, width), BF16),
            vmem((2, rows_of, fh), BF16),
            vmem((2 * nz * cap, width), BF16),
            vmem((2 * nz * cap, fh), BF16),
            vmem((2 * nz * cap, fh), BF16),
            vmem((nz * cap, width), F32),
            vmem((nz * cap, width), F32),
            vmem((nz * cap, width), F32),
            vmem((nz, 2 * cap, width // 2), BF16),
            vmem((nz, 2 * cap, width // 2), BF16),
            vmem((nx, ny, 2, rows_of, fh), BF16),
            vmem((nx, ny, 2, rows_of, fh), BF16),
            vmem((2, ny, rows_of, fh), BF16),
            vmem((2, nx, rows_of, fh), BF16),
            vmem((2, 2, ny, rows_of, fh), BF16),
            vmem((2, 2, nx, rows_of, fh), BF16),
            vmem((ny, 2, rows_of, fh), BF16),
            vmem((nx, 2, rows_of, fh), BF16),
            vmem((4, 2, rows_of, fh), BF16),
            vmem((4, 2, rows_of, fh), BF16),
            vmem((2, rows_of, fh), BF16),
            dma((7,)),
            dma((nz,)), dma((nz,)), dma((nz,)), dma((nz,)),
            dma((2,)), dma((2,)), dma((4, 4)), dma((4, 4)), dma((4, 4)), dma((4, 4)),
            dma((len(groups),)), dma((len(groups),)), dma((nz,)), dma((nz,)),
            dma((2, 6)), dma((2, 6)), dma((2, 8)), dma((2, 8)), dma((2,)),
        ],
        compiler_params=pltpu.CompilerParams(
            collective_id=0, has_side_effects=True, vmem_limit_bytes=60 * 1024 * 1024
        ),
    )(
        tokens, out_grad, probs.T, routes.T,
        w_gate.reshape(rows_of, ff), w_up.reshape(rows_of, ff), w_down.reshape(down_rows, width),
    )


def build(mesh, nx, ny, groups, cap):
    nz = mesh.shape["expert"]

    def local(*args):
        token_grad, gate_grad, up_grad = body(nx, ny, nz, groups, cap, *args)
        return token_grad.astype(BF16), gate_grad[None].astype(BF16), up_grad[None].astype(BF16)

    return jax.shard_map(
        local,
        mesh=mesh,
        in_specs=(P(("dp", "expert"), None),) * 4 + (P("expert", "dp", None),) * 3,
        out_specs=(P(("dp", "expert"), None), P("expert", "dp", None), P("expert", "dp", None)),
        check_vma=False,
    )


def solution(mesh):
    return build(mesh, 4, 4, (0, 4, 8, 12, 16), 24)
```
